256 devices in a mesh: bins: 64 (over y, x_hi, z), band: 4 (over x_lo, core).
Axes of the slice: x: 4 (x_hi: 2, x_lo: 2; x = x_hi * 2 + x_lo), y: 4, z: 8, core: 2. Of those that a mesh axis runs over, the one named last changes fastest.
Arguments:
- features: bfloat16 [2048, 64], P('bins'), may hold values from -6 to 6
- left_weight: bfloat16 [64, 64], replicated, may hold values from -0.75 to 0.75
- right_weight: bfloat16 [64, 64], replicated, may hold values from -0.75 to 0.75
- offset_embed: bfloat16 [64, 512], P(None, 'band'), may hold values from -4 to 4
- kernels: bfloat16 [2, 3, 3, 64, 64], replicated, may hold values from -0.4375 to 0.4375
- dilation: int32 [2], replicated, may hold values from 1 to 4, as said below
- cotangent: bfloat16 [2048, 64, 512], P('bins', None, 'band'), may hold values from -6 to 6
Outputs:
- pair_map: bfloat16 [2048, 64, 512], P('bins', None, 'band')
- grad_features: float32 [2048, 64], P('bins')
- grad_left: float32 [64, 64], replicated
- grad_right: float32 [64, 64], replicated
- grad_offset: float32 [64, 512], P(None, 'band')
- grad_kernels: float32 [2, 3, 3, 64, 64], replicated
The draws below stay inside these ranges and needn't reach their ends.
Inputs may be any that keep to these rules, and one draw needn't show every extreme that they name: Each entry is one layer's dilation; the largest entry equals 4.
All inputs are finite; a program needn't handle non-finite values.
Results may differ from the reference program's by a relative error of at most 0.02.
Values may be sent and summed in bfloat16 or wider, within the bound.
No kernel may reach another device: no remote copies, remote signals or barrier semaphores. Data moves between devices by JAX's collectives and lax.ppermute only.
A program may use at most 64 MiB of HBM per device.

```python
import math
import jax
import jax.numpy as jnp
from jax import lax

CHANNELS = 64
BAND = 512
LAYERS = 2
MAXDIL = 4
BINS = 2048


def draw_dilation(key, part):
    key = jax.random.fold_in(key, 11)
    first_key, second_key = jax.random.split(key)
    others = jax.random.randint(first_key, (LAYERS - 1,), 1, MAXDIL + 1, dtype=jnp.int32)
    values = jnp.concatenate([others, jnp.full((1,), MAXDIL, jnp.int32)])
    order = jax.random.permutation(second_key, LAYERS)
    return values[order]


def block_levels(stream_key, dims, shards, least, largest):
    level, own = 1.0, jax.random.fold_in(stream_key, 6)
    for axis_at, shards_of in shards:
        draws = jnp.exp(jax.random.uniform(jax.random.fold_in(own, axis_at), (shards_of,), jnp.float32, least / len(shards), largest / len(shards)))
        level = level * jnp.repeat(draws, dims[axis_at] // shards_of).reshape([-1 if axis == axis_at else 1 for axis in range(len(dims))])
    return level


def centred(own_key, dims, scale, most, cuts=(), held_as=jnp.bfloat16):
    drawn = jax.random.normal(own_key, dims, jnp.float32) * scale
    if len(cuts) > 0:
        drawn = block_levels(own_key, dims, cuts, -0.22, 0.18) * drawn
    return jnp.clip(drawn, min=-most, max=most).astype(held_as)


def setup_inputs(seed: int = 0) -> dict:
    keys = jax.random.split(jax.random.key(seed), 8)
    return {
        "features": centred(keys[0], (BINS, CHANNELS), 1.0, 6.0, ((0, 64),)),
        "left_weight": centred(keys[1], (CHANNELS, CHANNELS), CHANNELS ** -0.5, 0.75),
        "right_weight": centred(keys[2], (CHANNELS, CHANNELS), CHANNELS ** -0.5, 0.75),
        "offset_embed": centred(keys[3], (CHANNELS, BAND), 0.7, 4.0, ((1, 4),)),
        "kernels": centred(keys[4], (LAYERS, 3, 3, CHANNELS, CHANNELS), (3 * CHANNELS) ** -0.5, 0.4375),
        "dilation": draw_dilation(jax.random.fold_in(keys[7], 71), 0),
        "cotangent": centred(keys[6], (BINS, CHANNELS, BAND), 1.0, 6.0, ((0, 64), (2, 4))),
    }


def silu_slope(value):
    sigma = jax.nn.sigmoid(value)
    return sigma * (1.0 + value * (1.0 - sigma))

def tap_view(padded, row_start, col_start):
    return lax.dynamic_slice(padded, (row_start, jnp.int32(0), col_start), (BINS, CHANNELS, BAND))

def pad_map(state):
    return jnp.pad(state, ((MAXDIL, MAXDIL), (0, 0), (MAXDIL, MAXDIL)))

def reference(features, left_weight, right_weight, offset_embed, kernels, dilation, cotangent):
    left = jnp.dot(features, left_weight, preferred_element_type=jnp.float32).astype(jnp.bfloat16)
    right = jnp.dot(features, right_weight, preferred_element_type=jnp.float32).astype(jnp.bfloat16)
    right_ext = jnp.concatenate([right, jnp.zeros((BAND, CHANNELS), jnp.bfloat16)], 0)

    def lagged(offset):
        return lax.dynamic_slice(right_ext, (offset, jnp.int32(0)), (BINS, CHANNELS))
    sheared = jax.vmap(lagged)(jnp.arange(BAND, dtype=jnp.int32))
    sheared = jnp.transpose(sheared, (1, 2, 0))
    bin_ids = jnp.arange(BINS, dtype=jnp.int32)
    offset_ids = jnp.arange(BAND, dtype=jnp.int32)
    mask = (bin_ids[:, None] + offset_ids[None, :] < BINS).astype(jnp.float32)[:, None, :]
    summed = left.astype(jnp.float32)[:, :, None] + sheared.astype(jnp.float32) + offset_embed.astype(jnp.float32)[None]
    states = [(jax.nn.silu(summed) * mask).astype(jnp.bfloat16)]
    pres = []
    for layer in range(LAYERS):
        rate = dilation[layer]
        padded = pad_map(states[-1])
        total = jnp.zeros((BINS, CHANNELS, BAND), jnp.float32)
        for row_tap in range(3):
            for col_tap in range(3):
                view = tap_view(padded, MAXDIL + rate * (row_tap - 1), MAXDIL + rate * (col_tap - 1))
                total = total + jnp.einsum('icd,ce->ied', view.astype(jnp.float32), kernels[layer, row_tap, col_tap].astype(jnp.float32))
        pres.append(total)
        states.append((jax.nn.silu(total) * mask).astype(jnp.bfloat16))
    back = cotangent.astype(jnp.float32)
    kernel_grads = [None] * LAYERS
    for layer in reversed(range(LAYERS)):
        rate = dilation[layer]
        grad_pre = (back * mask * silu_slope(pres[layer])).astype(jnp.bfloat16)
        padded_state = pad_map(states[layer])
        padded_grad = pad_map(grad_pre)
        taps = []
        fresh = jnp.zeros((BINS, CHANNELS, BAND), jnp.float32)
        for row_tap in range(3):
            for col_tap in range(3):
                view = tap_view(padded_state, MAXDIL + rate * (row_tap - 1), MAXDIL + rate * (col_tap - 1))
                taps.append(jnp.einsum('icd,ied->ce', view.astype(jnp.float32), grad_pre.astype(jnp.float32)))
                mirror = tap_view(padded_grad, MAXDIL - rate * (row_tap - 1), MAXDIL - rate * (col_tap - 1))
                fresh = fresh + jnp.einsum('ied,ce->icd', mirror.astype(jnp.float32), kernels[layer, row_tap, col_tap].astype(jnp.float32))
        kernel_grads[layer] = jnp.stack(taps).reshape(3, 3, CHANNELS, CHANNELS)
        back = fresh
    grad_sum = back * mask * silu_slope(summed)
    left_grad = lax.optimization_barrier(jnp.sum(grad_sum, axis=2))
    offset_sum = lax.optimization_barrier(jnp.sum(grad_sum, axis=0))

    def spread(offset, total):
        column = lax.dynamic_index_in_dim(grad_sum, offset, 2, keepdims=False)
        current = lax.dynamic_slice(total, (offset, jnp.int32(0)), (BINS, CHANNELS))
        return lax.dynamic_update_slice(total, current + column, (offset, jnp.int32(0)))
    right_grad = lax.fori_loop(jnp.int32(0), jnp.int32(BAND), spread, jnp.zeros((BINS + BAND, CHANNELS), jnp.float32))[:BINS]
    highest = lax.Precision.HIGHEST
    grad_features = (jnp.dot(left_grad, left_weight.astype(jnp.float32).T, precision=highest) + jnp.dot(right_grad, right_weight.astype(jnp.float32).T, precision=highest)) / math.sqrt(BAND)
    whole_scale = math.sqrt(BINS * BAND)
    grad_left = jnp.dot(features.astype(jnp.float32).T, left_grad, precision=highest) / whole_scale
    grad_right = jnp.dot(features.astype(jnp.float32).T, right_grad, precision=highest) / whole_scale
    grad_offset = offset_sum / math.sqrt(BINS)
    grad_kernels = jnp.stack(kernel_grads) / whole_scale
    return (states[-1], grad_features, grad_left, grad_right, grad_offset, grad_kernels)
```

```python
import functools
import math

import jax
import jax.numpy as jnp
from jax import lax
from jax.experimental import pallas as pl
from jax.experimental.pallas import tpu as pltpu
from jax.sharding import PartitionSpec as P

LAYERS = 2
MAXDIL = 4
F32 = jnp.float32
BF16 = jnp.bfloat16
WIDE = 256
RIM0 = 16
RIM1 = 12
RIM2 = 8
RIM3 = 4
LIMIT = 56 * 1024 * 1024


def sigmoid(value):
    return 0.5 * jnp.tanh(0.5 * value) + 0.5


def turned(value, amount):
    return pltpu.roll(value, amount, 1)


def row_mask(bin_id, first_offset, total_bins, total_band, lanes):
    lane = lax.broadcasted_iota(jnp.int32, (1, lanes), 1)
    offset = first_offset + jnp.where(lane < 192, lane, lane - WIDE)
    top = jnp.minimum(total_band, total_bins - bin_id)
    top = jnp.where(bin_id >= 0, top, 0)
    return jnp.where((offset >= 0) & (offset < top), 1.0, 0.0).astype(F32)


def forward_kernel(
    rows, channels, total_bins, total_band,
    place, dil, lo, own, hi, w0, w1, w2, w3, w4, w5, w6, lw, rw, emb_lo, emb, emb_hi, taps,
    s0, s1, slope_s, slope0, proj,
):
    c = channels
    first_bin = place[0] * rows
    group = emb.shape[1]
    first_offset = place[1] * group
    fw = jnp.concatenate([w0[...], w1[...], w2[...], w3[...], w4[...], w5[...], w6[...]], 0)
    right = jnp.dot(fw, rw[...], preferred_element_type=F32).astype(BF16).astype(F32)
    near = jnp.concatenate([lo[...], own[...], hi[...]], 0)
    left = jnp.dot(near, lw[...], preferred_element_type=F32).astype(BF16).astype(F32)
    right = jnp.concatenate([right, jnp.zeros((WIDE - right.shape[0], c), F32)], 0)
    left = jnp.concatenate([left, jnp.zeros((WIDE - left.shape[0], c), F32)], 0)
    proj[...] = jnp.concatenate([right, left], 1).T
    lane = lax.broadcasted_iota(jnp.int32, (1, group), 1)
    beside = jnp.where(lane < group // 2, emb_hi[...].astype(F32), emb_lo[...].astype(F32))
    embed = jnp.concatenate([emb[...].astype(F32), beside], 1)

    def state_row(row, carry):
        bin_id = first_bin - RIM0 + row
        lag = turned(proj[0:c, :], WIDE - RIM0 - row)
        mine = turned(proj[c : 2 * c, :], WIDE - rows + RIM0 - row)[:, 0:1]
        summed = mine + lag + embed
        sig = sigmoid(summed)
        mask = row_mask(bin_id, first_offset, total_bins, total_band, WIDE)
        at = pl.ds(pl.multiple_of(row * c, c), c)
        s0[at, :] = (summed * sig * mask).astype(BF16)

        @pl.when((row >= RIM0) & (row < RIM0 + rows))
        def _():
            slope = sig * (1.0 + summed * (1.0 - sig)) * mask
            slope_s[pl.ds(pl.multiple_of((row - RIM0) * c, c), c), :] = slope[:, 0:group]

        return carry

    lax.fori_loop(0, rows + 2 * RIM0, state_row, 0)

    rate = dil[0]

    def layer_row(row, carry):
        bin_id = first_bin - RIM1 + row
        base = row + RIM0 - RIM1
        view = jnp.concatenate(
            [s0[pl.ds(pl.multiple_of((base + rate * k) * c, c), c), :] for k in (-1, 0, 1)], 0
        )
        parts = jnp.dot(taps[0], view, preferred_element_type=F32)
        pre = (
            turned(parts[0:c], rate) + parts[c : 2 * c] + turned(parts[2 * c : 3 * c], WIDE - rate)
        )
        sig = sigmoid(pre)
        mask = row_mask(bin_id, first_offset, total_bins, total_band, WIDE)
        at = pl.ds(pl.multiple_of(row * c, c), c)
        s1[at, :] = (pre * sig * mask).astype(BF16)
        slope0[at, :] = sig * (1.0 + pre * (1.0 - sig)) * mask
        return carry

    lax.fori_loop(0, rows + 2 * RIM1, layer_row, 0)


def backward_kernel(
    rows, channels, total_bins, total_band,
    place, dil, s0, s1, slope_s, slope0, cot, taps, back_taps, lo, own, w1, w2, w3, w4, w5, lw, rw,
    pair_map, payload, feature_left, feature_right,
    g1, g0, sums, edge,
):
    c = channels
    first_bin = place[0] * rows
    group = pair_map.shape[2]
    first_offset = place[1] * group
    rate0, rate1 = dil[0], dil[1]

    def layer_row(row, carry):
        bin_id = first_bin - RIM2 + row
        base = row + RIM1 - RIM2
        view = jnp.concatenate(
            [s1[pl.ds(pl.multiple_of((base + rate1 * k) * c, c), c), :] for k in (-1, 0, 1)], 0
        )
        parts = jnp.dot(taps[1], view, preferred_element_type=F32)
        pre = (
            turned(parts[0:c], rate1)
            + parts[c : 2 * c]
            + turned(parts[2 * c : 3 * c], WIDE - rate1)
        )
        sig = sigmoid(pre)
        mask = row_mask(bin_id, first_offset, total_bins, total_band, WIDE)
        slope = sig * (1.0 + pre * (1.0 - sig)) * mask
        g1[pl.ds(pl.multiple_of(row * c, c), c), :] = (cot[row].astype(F32) * slope).astype(BF16)

        @pl.when((row >= RIM2) & (row < RIM2 + rows))
        def _():
            pair_map[row - RIM2] = (pre * sig * mask).astype(BF16)[:, 0:group]

        return carry

    lax.fori_loop(0, rows + 2 * RIM2, layer_row, 0)

    def back_parts(layer, rate, grads, base):
        view = jnp.concatenate(
            [grads[pl.ds(pl.multiple_of((base - rate * k) * c, c), c), :] for k in (-1, 0, 1)], 0
        )
        parts = jnp.dot(back_taps[layer], view, preferred_element_type=F32)
        return (
            turned(parts[0:c], WIDE - rate) + parts[c : 2 * c] + turned(parts[2 * c : 3 * c], rate)
        )

    def back_row(row, carry):
        back = back_parts(1, rate1, g1, row + RIM2 - RIM3)
        at = pl.ds(pl.multiple_of((row + RIM1 - RIM3) * c, c), c)
        g0[pl.ds(pl.multiple_of(row * c, c), c), :] = (back * slope0[at, :]).astype(BF16)
        return carry

    lax.fori_loop(0, rows + 2 * RIM3, back_row, 0)

    def tap_sums(rate, state, rim_s, grads, rim_g):
        def one(row, total):
            view = jnp.concatenate(
                [
                    state[pl.ds(pl.multiple_of((row + rim_s + rate * k) * c, c), c), :]
                    for k in (-1, 0, 1)
                ],
                0,
            )
            grad = grads[pl.ds(pl.multiple_of((row + rim_g) * c, c), c), 0:group].astype(F32)
            grad = jnp.concatenate([grad, jnp.zeros((c, WIDE - group), F32)], 1)
            shifted = jnp.concatenate(
                [turned(grad, WIDE - rate), grad, turned(grad, rate)], 0
            ).astype(BF16)
            return total + lax.dot_general(
                view, shifted, (((1,), (1,)), ((), ())), preferred_element_type=F32
            )

        return lax.fori_loop(0, rows, one, jnp.zeros((3 * c, 3 * c), F32))

    total1 = tap_sums(rate1, s1, RIM1, g1, RIM2)
    payload[3 * c : 6 * c, :] = total1[:, 0:128]
    edge[...] = total1[:, 128 : 3 * c]
    total0 = tap_sums(rate0, s0, RIM0, g0, RIM3)
    payload[0 : 3 * c, :] = total0[:, 0:128]
    payload[6 * c : 9 * c, :] = jnp.concatenate([total0[:, 128 : 3 * c], edge[...]], 1)

    lane = lax.broadcasted_iota(jnp.int32, (1, 128), 1)
    sums[...] = jnp.zeros_like(sums)

    def last_row(row, carry):
        back = back_parts(0, rate0, g0, row + RIM3)
        at = pl.ds(pl.multiple_of(row * c, c), c)
        grad = back[:, 0:group] * slope_s[at, :]
        sums[:, 0:128] += jnp.where(lane == row, jnp.sum(grad, axis=1, keepdims=True), 0.0)
        wide = jnp.concatenate([grad, jnp.zeros((c, WIDE - group), F32)], 1)
        sums[:, 128 : 128 + WIDE] += turned(wide, row)
        sums[:, 128 + WIDE : 256 + WIDE] += grad
        return carry

    lax.fori_loop(0, rows, last_row, 0)

    highest = lax.Precision.HIGHEST
    both = sums[:, 0 : 128 + WIDE]
    both = jnp.concatenate([both, jnp.zeros_like(both)], 0).T
    left_grad = both[0:rows, 0:c]
    right_grad = both[128 : 128 + rows + group, 0:c]
    window = jnp.concatenate([w1[...], w2[...], w3[...], w4[...], w5[...]], 0).astype(F32)
    feats = jnp.concatenate([own[...].astype(F32), window], 0)
    feats = jnp.concatenate([feats, jnp.zeros((WIDE - feats.shape[0], c), F32)], 0)
    feats = jnp.concatenate([feats, jnp.zeros_like(feats)], 1).T[0:c]
    grad_left = jnp.dot(feats[:, 0:rows], left_grad, precision=highest, preferred_element_type=F32)
    grad_right = jnp.dot(
        feats[:, rows : 2 * rows + group], right_grad, precision=highest,
        preferred_element_type=F32,
    )
    payload[9 * c : 10 * c, :] = jnp.concatenate([grad_left, grad_right], 1)
    payload[10 * c :, :] = jnp.zeros((payload.shape[0] - 10 * c, 128), F32)
    at = pl.ds(pl.multiple_of((10 + place[1]) * c, c), c)
    payload[at, :] = sums[:, 128 + WIDE : 256 + WIDE]
    transposed = (((1,), (1,)), ((), ()))
    feature_left[...] = lax.dot_general(
        left_grad, lw[...].astype(F32), transposed, precision=highest, preferred_element_type=F32
    )
    feature_right[...] = lax.dot_general(
        right_grad, rw[...].astype(F32), transposed, precision=highest, preferred_element_type=F32
    ).reshape(feature_right.shape)


def unpack_kernel(channels, whole_scale, offset_scale, place, total, left, right, offset, kernels):
    c = channels
    for layer in range(2):
        for p in range(3):
            main = total[(3 * layer + p) * c : (3 * layer + p + 1) * c, :] * whole_scale
            rest = total[(6 + p) * c : (7 + p) * c, :] * whole_scale
            kernels[layer, p, 0] = main[:, 0:c]
            kernels[layer, p, 1] = main[:, c : 2 * c]
            kernels[layer, p, 2] = rest[:, layer * c : (layer + 1) * c]
    both = total[9 * c : 10 * c, :] * whole_scale
    left[...] = both[:, 0:c]
    right[...] = both[:, c : 2 * c]
    at = pl.ds(pl.multiple_of((10 + place[1]) * c, c), c)
    offset[...] = total[at, :] * offset_scale


def per_device(features, left_weight, right_weight, offset_embed, kernels, dilation, cotangent):
    rows, c = features.shape
    group = offset_embed.shape[1]
    bins, band = lax.axis_size("bins"), lax.axis_size("band")
    devices = bins * band
    total_bins, total_band = rows * bins, group * band
    blocks = group // rows
    every = ("bins", "band")
    place = jnp.stack([lax.axis_index("bins"), lax.axis_index("band")]).astype(jnp.int32)

    def joint(bin_step, band_step, skew=0):
        route = []
        for i in range(bins):
            for b in range(band):
                i2, b2 = i + bin_step + skew * b, b + band_step
                if 0 <= i2 < bins and 0 <= b2 < band:
                    route.append((i2 * band + b2, i * band + b))
        return route

    def fetch(block, bin_step, band_step, skew=0):
        return lax.ppermute(block, every, joint(bin_step, band_step, skew))

    def deliver(block, bin_step, skew):
        route = [(target, source) for source, target in joint(bin_step, 0, skew)]
        return lax.ppermute(block, every, route)

    window = [fetch(features, k, 0, blocks) for k in range(-1, blocks + 2)]
    lo, hi = fetch(features, -1, 0), fetch(features, 1, 0)
    emb_lo, emb_hi = fetch(offset_embed, 0, -1), fetch(offset_embed, 0, 1)
    cot_rows = jnp.concatenate(
        [fetch(cotangent[rows - RIM2 :], -1, 0), cotangent, fetch(cotangent[:RIM2], 1, 0)], 0
    )
    cot_lo = fetch(cot_rows[:, :, group - RIM2 :], 0, -1)
    cot_hi = fetch(cot_rows[:, :, :RIM2], 0, 1)
    gap = jnp.zeros((rows + 2 * RIM2, c, WIDE - group - 2 * RIM2), BF16)
    cot = jnp.concatenate([cot_rows, cot_hi, gap, cot_lo], 2)

    taps = jnp.transpose(kernels, (0, 2, 4, 1, 3)).reshape(LAYERS, 3 * c, 3 * c)
    back_taps = jnp.transpose(kernels, (0, 2, 3, 1, 4)).reshape(LAYERS, 3 * c, 3 * c)

    smem = pl.BlockSpec(memory_space=pltpu.SMEM)
    vmem = pl.BlockSpec(memory_space=pltpu.VMEM)
    s0, s1, slope_s, slope0 = pl.pallas_call(
        functools.partial(forward_kernel, rows, c, total_bins, total_band),
        out_shape=(
            jax.ShapeDtypeStruct(((rows + 2 * RIM0) * c, WIDE), BF16),
            jax.ShapeDtypeStruct(((rows + 2 * RIM1) * c, WIDE), BF16),
            jax.ShapeDtypeStruct((rows * c, group), F32),
            jax.ShapeDtypeStruct(((rows + 2 * RIM1) * c, WIDE), F32),
        ),
        in_specs=[smem] * 2 + [vmem] * 16,
        out_specs=(vmem,) * 4,
        scratch_shapes=[pltpu.VMEM((2 * c, WIDE), F32)],
        compiler_params=pltpu.CompilerParams(vmem_limit_bytes=LIMIT),
        name="forward",
    )(
        place, dilation, lo, features, hi, *window, left_weight, right_weight,
        emb_lo, offset_embed, emb_hi, taps,
    )
    slots = 4 * devices
    pair_map, payload, feature_left, feature_right = pl.pallas_call(
        functools.partial(backward_kernel, rows, c, total_bins, total_band),
        out_shape=(
            jax.ShapeDtypeStruct((rows, c, group), BF16),
            jax.ShapeDtypeStruct((slots, 128), F32),
            jax.ShapeDtypeStruct((rows, c), F32),
            jax.ShapeDtypeStruct((blocks + 1, rows, c), F32),
        ),
        in_specs=[smem] * 2 + [vmem] * 16,
        out_specs=(vmem,) * 4,
        scratch_shapes=[
            pltpu.VMEM(((rows + 2 * RIM2) * c, WIDE), BF16),
            pltpu.VMEM(((rows + 2 * RIM3) * c, WIDE), BF16),
            pltpu.VMEM((c, 256 + WIDE), F32),
            pltpu.VMEM((3 * c, 3 * c - 128), F32),
        ],
        compiler_params=pltpu.CompilerParams(vmem_limit_bytes=LIMIT),
        name="backward",
    )(
        place, dilation, s0, s1, slope_s, slope0, cot, taps, back_taps, lo, features,
        *window[1:6], left_weight, right_weight,
    )
    shares = lax.all_to_all(payload.reshape(devices, 4, 128), every, 0, 0, tiled=True)
    feature_sum = feature_left
    for k in range(blocks + 1):
        feature_sum = feature_sum + deliver(feature_right[k], k, blocks)
    feature_all = feature_sum
    for step in range(1, band):
        route = [(b, (b + step) % band) for b in range(band)]
        feature_all = feature_all + lax.ppermute(feature_sum, "band", route)
    share = jnp.broadcast_to(jnp.sum(shares, axis=0, keepdims=True), shares.shape)
    total = lax.all_to_all(share, every, 0, 0, tiled=True).reshape(slots, 128)
    whole_scale = 1.0 / math.sqrt(total_bins * total_band)
    grad_left, grad_right, grad_offset, grad_kernels = pl.pallas_call(
        functools.partial(unpack_kernel, c, whole_scale, 1.0 / math.sqrt(total_bins)),
        out_shape=(
            jax.ShapeDtypeStruct((c, c), F32),
            jax.ShapeDtypeStruct((c, c), F32),
            jax.ShapeDtypeStruct((c, group), F32),
            jax.ShapeDtypeStruct((LAYERS, 3, 3, c, c), F32),
        ),
        in_specs=[smem, vmem],
        out_specs=(vmem,) * 4,
        compiler_params=pltpu.CompilerParams(vmem_limit_bytes=LIMIT),
        name="unpack",
    )(place, total)
    return (
        pair_map,
        feature_all / math.sqrt(total_band),
        grad_left,
        grad_right,
        grad_offset,
        grad_kernels,
    )


def solution(mesh):
    return jax.shard_map(
        per_device,
        mesh=mesh,
        in_specs=(P("bins", None), P(), P(), P(None, "band"), P(), P(), P("bins", None, "band")),
        out_specs=(P("bins", None, "band"), P("bins", None), P(), P(), P(None, "band"), P()),
        check_vma=False,
    )
```

```python
import functools
import math

import jax
import jax.numpy as jnp
from jax import lax
from jax.experimental import pallas as pl
from jax.experimental.pallas import tpu as pltpu
from jax.sharding import PartitionSpec as P

LAYERS = 2
F32 = jnp.float32
BF16 = jnp.bfloat16
HALF = 128
WIDE = 256
RIM0 = 16
RIM1 = 12
RIM2 = 8
RIM3 = 4
CHUNK = 32
LIMIT = 56 * 1024 * 1024
VMEM = pl.BlockSpec(memory_space=pltpu.VMEM)
SMEM = pl.BlockSpec(memory_space=pltpu.SMEM)


def sigmoid(value):
    return 0.5 * jnp.tanh(0.5 * value) + 0.5


def lanes_of(width):
    return lax.broadcasted_iota(jnp.int32, (1, width), 1)


def up(value, amount):
    first = lanes_of(HALF) < amount
    a = pltpu.roll(value[:, :HALF], amount, 1)
    b = pltpu.roll(value[:, HALF:], amount, 1)
    return jnp.concatenate([jnp.where(first, b, a), jnp.where(first, a, b)], 1)


def down(value, amount):
    first = lanes_of(HALF) < HALF - amount
    a = pltpu.roll(value[:, :HALF], HALF - amount, 1)
    b = pltpu.roll(value[:, HALF:], HALF - amount, 1)
    return jnp.concatenate([jnp.where(first, a, b), jnp.where(first, b, a)], 1)


def sweep(count, held, body):
    def step(at, carry):
        for k in range(held):
            body(at * held + k)
        return carry

    lax.fori_loop(0, count // held, step, 0)


def middle_kernel(
    rows, c, total_bins, total_band,
    place, dil, feats, cot_up, cot, cot_down, from_lo, from_hi, emb, lw, rw, taps, back_taps,
    pair_map, payload,
    proj, embed, s0, s1, slope_s, slope0, wide_cot, pairs, g1, g0, sums, edge,
):
    bins = total_bins // rows
    group = emb.shape[1]
    span = group // rows
    first_bin = place[0] * rows
    first_offset = place[1] * group
    rate0, rate1 = dil[0], dil[1]
    edges = from_lo.shape[0] - c

    def rows_at(row, count=1):
        return pl.ds(pl.multiple_of(row * c, c), count * c)

    def mask_of(bin_id):
        lane = lanes_of(WIDE)
        offset = first_offset + jnp.where(lane < 192, lane, lane - WIDE)
        top = jnp.minimum(total_band, total_bins - bin_id)
        top = jnp.where(bin_id >= 0, top, 0)
        return jnp.where((offset >= 0) & (offset < top), 1.0, 0.0).astype(F32)

    def block(index):
        inside = (index >= 0) & (index < bins)
        half = feats[jnp.clip(index, 0, bins - 1)].astype(F32) * jnp.where(inside, 1.0, 0.0)
        return jnp.concatenate([half[:, :c], half[:, c:]], 0)

    base = place[0] + place[1] * span
    near = [block(place[0] + k) for k in (-1, 0, 1)]
    window = [block(base + k) for k in range(-1, span + 2)]
    filler = jnp.zeros((WIDE - (span + 3) * rows, c), F32)
    fw = jnp.concatenate(window + [filler], 0).astype(BF16)
    right = jnp.dot(fw, rw[...], preferred_element_type=F32).astype(BF16).astype(F32)
    filler = jnp.zeros((WIDE - 3 * rows, c), F32)
    fl = jnp.concatenate(near + [filler], 0).astype(BF16)
    left = jnp.dot(fl, lw[...], preferred_element_type=F32).astype(BF16).astype(F32)
    proj[...] = jnp.concatenate([right, left], 1).T
    beside = jnp.where(
        lanes_of(HALF) < HALF // 2, from_hi[edges:, :].astype(F32), from_lo[edges:, :].astype(F32)
    )
    embed[...] = jnp.concatenate([emb[...].astype(F32), beside], 1)
    wide_cot[0:RIM2] = cot_up[...]
    wide_cot[RIM2 : RIM2 + rows] = cot[...]
    wide_cot[RIM2 + rows :] = cot_down[...]

    def state_row(row):
        lag = down(proj[0:c, :], RIM0 + row)
        mine = pltpu.roll(proj[c : 2 * c, 0:HALF], HALF - RIM0 - row, 1)[:, 0:1]
        summed = mine + lag + embed[...]
        sig = sigmoid(summed)
        mask = mask_of(first_bin - RIM0 + row)
        s0[rows_at(row), :] = (summed * sig * mask).astype(BF16)
        slope = sig * (1.0 + summed * (1.0 - sig)) * mask
        slope_s[rows_at(row), :] = slope[:, 0:HALF]

    sweep(rows + 2 * RIM0, 16, state_row)

    def convolved(weights, source, base_row, rate):
        view = jnp.concatenate([source[rows_at(base_row + rate * k), :] for k in (-1, 0, 1)], 0)
        parts = jnp.dot(weights, view, preferred_element_type=F32)
        return parts[0:c], parts[c : 2 * c], parts[2 * c : 3 * c]

    def layer_row0(row):
        a, b, d = convolved(taps[0], s0, row + RIM0 - RIM1, rate0)
        pre = up(a, rate0) + b + down(d, rate0)
        sig = sigmoid(pre)
        mask = mask_of(first_bin - RIM1 + row)
        s1[rows_at(row), :] = (pre * sig * mask).astype(BF16)
        slope0[rows_at(row), :] = sig * (1.0 + pre * (1.0 - sig)) * mask

    sweep(rows + 2 * RIM1, 28, layer_row0)

    def layer_row1(row):
        a, b, d = convolved(taps[1], s1, row + RIM1 - RIM2, rate1)
        pre = up(a, rate1) + b + down(d, rate1)
        sig = sigmoid(pre)
        mask = mask_of(first_bin - RIM2 + row)
        slope = sig * (1.0 + pre * (1.0 - sig)) * mask
        pairs[row] = (pre * sig * mask)[:, 0:HALF].astype(BF16)
        tile = rows_at(row // 16)
        turn = (row % 16) * RIM2
        hi = pltpu.roll(from_hi[tile, :].astype(F32), (HALF - turn) % HALF, 1)
        lo = pltpu.roll(from_lo[tile, :].astype(F32), HALF - RIM2 - turn, 1)
        rim = jnp.where(lanes_of(HALF) < HALF // 2, hi, lo)
        grad = jnp.concatenate([wide_cot[row].astype(F32), rim], 1)
        g1[rows_at(row), :] = (grad * slope).astype(BF16)

    sweep(rows + 2 * RIM2, 16, layer_row1)
    pair_map[...] = pairs[RIM2 : RIM2 + rows]

    def back_row(row):
        a, b, d = convolved(back_taps[1], g1, row + RIM2 - RIM3, -rate1)
        back = down(a, rate1) + b + up(d, rate1)
        slope = slope0[rows_at(row + RIM1 - RIM3), :]
        g0[rows_at(row), :] = (back * slope).astype(BF16)

    sweep(rows + 2 * RIM3, 40, back_row)

    def tap_sums(rate, state, rim_s, grads, rim_g):
        lane = lanes_of(HALF)

        def views(row):
            view = [state[rows_at(row + rim_s + rate * k), :] for k in (-1, 0, 1)]
            grad = grads[rows_at(row + rim_g), 0:HALF].astype(F32)
            low = pltpu.roll(grad, HALF - rate, 1)
            high = pltpu.roll(grad, rate, 1)
            low0 = jnp.where(lane < HALF - rate, low, 0.0)
            high1 = jnp.where(lane < rate, high, 0.0)
            first = jnp.concatenate([low0, grad, high - high1], 0)
            second = jnp.concatenate([low - low0, jnp.zeros_like(grad), high1], 0)
            return jnp.concatenate(view, 0), jnp.concatenate([first, second], 1).astype(BF16)

        def step(at, total):
            both = [views(at * CHUNK + k) for k in range(CHUNK)]
            view = jnp.concatenate([v for v, _ in both], 1)
            grad = jnp.concatenate([g for _, g in both], 1)
            return total + lax.dot_general(
                view, grad, (((1,), (1,)), ((), ())), preferred_element_type=F32
            )

        return lax.fori_loop(0, rows // CHUNK, step, jnp.zeros((3 * c, 3 * c), F32))

    def place_rows(start, value):
        count = value.shape[0] // 4
        payload[start // 4 : start // 4 + count, 4:8, :] = value.reshape(count, 4, HALF).astype(
            BF16
        )

    total1 = tap_sums(rate1, s1, RIM1, g1, RIM2)
    place_rows(3 * c, total1[:, 0:HALF])
    edge[...] = total1[:, HALF : 3 * c]
    total0 = tap_sums(rate0, s0, RIM0, g0, RIM3)
    place_rows(0, total0[:, 0:HALF])
    place_rows(6 * c, jnp.concatenate([total0[:, HALF : 3 * c], edge[...]], 1))

    sums[...] = jnp.zeros_like(sums)
    lane = lanes_of(HALF)

    def last_row(row):
        a, b, d = convolved(back_taps[0], g0, row + RIM3, -rate0)
        back = (down(a, rate0) + b + up(d, rate0))[:, 0:HALF]
        grad = back * slope_s[rows_at(row + RIM0), :]
        total = jnp.sum(grad, axis=1, keepdims=True)
        sums[:, 0:HALF] += jnp.where(lane == row, total, 0.0)
        turned = pltpu.roll(grad, row, 1)
        wrapped = jnp.where(lane < row, turned, 0.0)
        sums[:, HALF : 2 * HALF] += turned - wrapped
        sums[:, 2 * HALF : 3 * HALF] += wrapped
        sums[:, 3 * HALF : 4 * HALF] += grad

    sweep(rows, 16, last_row)

    highest = lax.Precision.HIGHEST
    both = sums[:, 0 : 3 * HALF]
    both = jnp.concatenate([both, jnp.zeros_like(both)], 0).T
    left_grad = both[0:rows, 0:c]
    right_grad = both[HALF : HALF + rows + group, 0:c]
    fwin = jnp.concatenate([near[1]] + window[1 : span + 2], 0)
    fwin = jnp.concatenate([fwin, jnp.zeros((WIDE - fwin.shape[0], c), F32)], 0)
    fwin = jnp.concatenate([fwin, jnp.zeros_like(fwin)], 1).T[0:c]
    grad_left = jnp.dot(fwin[:, 0:rows], left_grad, precision=highest, preferred_element_type=F32)
    grad_right = jnp.dot(
        fwin[:, rows : 2 * rows + group], right_grad, precision=highest, preferred_element_type=F32
    )
    place_rows(9 * c, jnp.concatenate([grad_left, grad_right], 1))
    spare = payload.shape[0] - 10 * c // 4
    payload[10 * c // 4 :, 4:8, :] = jnp.zeros((spare, 4, HALF), BF16)
    at = pl.ds((10 * c + place[1] * c) // 4, c // 4)
    payload[at, 4:8, :] = sums[:, 3 * HALF : 4 * HALF].reshape(c // 4, 4, HALF).astype(BF16)

    transposed = (((1,), (1,)), ((), ()))
    feature_left = lax.dot_general(
        left_grad, lw[...].astype(F32), transposed, precision=highest, preferred_element_type=F32
    )
    feature_right = lax.dot_general(
        right_grad, rw[...].astype(F32), transposed, precision=highest, preferred_element_type=F32
    )
    payload[:, 0:4, :] = jnp.zeros((payload.shape[0], 4, HALF), BF16)

    def packed(value):
        return jnp.concatenate([value[0 : rows // 2], value[rows // 2 :]], 1).reshape(4, 4, HALF)

    mine = pl.ds(place[0] * 4, 4)
    payload[mine, 0:4, :] = packed(feature_left).astype(BF16)
    for k in range(span + 1):
        part = packed(feature_right[k * rows : (k + 1) * rows])

        @pl.when(base + k < bins)
        def _():
            target = pl.ds((base + k) * 4, 4)
            old = payload[target, 0:4, :].astype(F32)
            payload[target, 0:4, :] = (old + part).astype(BF16)


def middle(rows, c, group, total_bins, total_band, devices, args):
    tall = lambda rim: (rows + 2 * rim) * c
    return pl.pallas_call(
        functools.partial(middle_kernel, rows, c, total_bins, total_band),
        out_shape=(
            jax.ShapeDtypeStruct((rows, c, group), BF16),
            jax.ShapeDtypeStruct((devices, 8, HALF), BF16),
        ),
        in_specs=[SMEM] * 2 + [VMEM] * (len(args) - 2),
        out_specs=(VMEM,) * 2,
        scratch_shapes=[
            pltpu.VMEM((2 * c, WIDE), F32),
            pltpu.VMEM((c, WIDE), F32),
            pltpu.VMEM((tall(RIM0), WIDE), BF16),
            pltpu.VMEM((tall(RIM1), WIDE), BF16),
            pltpu.VMEM((tall(RIM0), HALF), F32),
            pltpu.VMEM((tall(RIM1), WIDE), F32),
            pltpu.VMEM((rows + 2 * RIM2, c, HALF), BF16),
            pltpu.VMEM((rows + 2 * RIM2, c, HALF), BF16),
            pltpu.VMEM((tall(RIM2), WIDE), BF16),
            pltpu.VMEM((tall(RIM3), WIDE), BF16),
            pltpu.VMEM((c, 4 * HALF), F32),
            pltpu.VMEM((3 * c, 3 * c - HALF), F32),
        ],
        compiler_params=pltpu.CompilerParams(vmem_limit_bytes=LIMIT),
        name="middle",
    )(*args)


def edge_kernel(rows, c, cot_up, cot, cot_down, emb, to_lo, to_hi):
    lane = lanes_of(HALF)
    count = rows + 2 * RIM2
    for tile in range(count // 16):
        low = jnp.zeros((c, HALF), F32)
        high = jnp.zeros((c, HALF), F32)
        for k in range(16):
            row = tile * 16 + k
            if row < RIM2:
                value = cot_up[row]
            elif row < RIM2 + rows:
                value = cot[row - RIM2]
            else:
                value = cot_down[row - RIM2 - rows]
            value = value.astype(F32)
            here = (lane >= RIM2 * k) & (lane < RIM2 * (k + 1))
            low = jnp.where(here, pltpu.roll(value, RIM2 * k, 1), low)
            high = jnp.where(here, pltpu.roll(value, RIM2 * (k + 1) % HALF, 1), high)
        to_lo[tile * c : (tile + 1) * c, :] = low.astype(BF16)
        to_hi[tile * c : (tile + 1) * c, :] = high.astype(BF16)
    to_lo[count // 16 * c :, :] = emb[...]
    to_hi[count // 16 * c :, :] = emb[...]


def share_kernel(parts, share, features):
    total = jnp.sum(parts[...].astype(F32), axis=0)
    features[...] = total[0:4]
    share[...] = jnp.broadcast_to(total[4:8].astype(BF16)[None], share.shape)


def unpack_kernel(c, whole_scale, offset_scale, place, total, left, right, offset, kernels):
    def piece(start):
        value = total[start // 4 : (start + c) // 4].astype(F32)
        return value.reshape(c, HALF)

    for p in range(3):
        rest = piece((6 + p) * c) * whole_scale
        for layer in range(2):
            main = piece((3 * layer + p) * c) * whole_scale
            kernels[layer, p, 0] = main[:, 0:c]
            kernels[layer, p, 1] = main[:, c : 2 * c]
            kernels[layer, p, 2] = rest[:, layer * c : (layer + 1) * c]
    both = piece(9 * c) * whole_scale
    left[...] = both[:, 0:c]
    right[...] = both[:, c : 2 * c]
    at = pl.ds((10 * c + place[1] * c) // 4, c // 4)
    offset[...] = total[at].astype(F32).reshape(c, HALF) * offset_scale


def per_device(features, left_weight, right_weight, offset_embed, kernels, dilation, cotangent):
    rows, c = features.shape
    group = offset_embed.shape[1]
    bins, band = lax.axis_size("bins"), lax.axis_size("band")
    devices = bins * band
    total_bins, total_band = rows * bins, group * band
    every = ("bins", "band")
    place = jnp.stack([lax.axis_index("bins"), lax.axis_index("band")]).astype(jnp.int32)

    def beside(block, axis, step):
        count = lax.axis_size(axis)
        route = [(i + step, i) for i in range(count) if 0 <= i + step < count]
        return lax.ppermute(block, axis, route)

    packed = jnp.concatenate([features[: rows // 2], features[rows // 2 :]], 1)
    feats = lax.all_to_all(
        jnp.broadcast_to(packed[None], (bins,) + packed.shape), "bins", 0, 0, tiled=True
    )
    cot_up = beside(cotangent[rows - RIM2 :], "bins", -1)
    cot_down = beside(cotangent[:RIM2], "bins", 1)
    edge_shape = jax.ShapeDtypeStruct(((rows + 2 * RIM2) // 16 * c + c, HALF), BF16)
    to_lo, to_hi = pl.pallas_call(
        functools.partial(edge_kernel, rows, c),
        out_shape=(edge_shape, edge_shape),
        in_specs=[VMEM] * 4,
        out_specs=(VMEM,) * 2,
        compiler_params=pltpu.CompilerParams(vmem_limit_bytes=LIMIT),
        name="edges",
    )(cot_up, cotangent, cot_down, offset_embed)
    from_lo = beside(to_hi, "band", -1)
    from_hi = beside(to_lo, "band", 1)

    taps = jnp.transpose(kernels, (0, 2, 4, 1, 3)).reshape(LAYERS, 3 * c, 3 * c)
    back_taps = jnp.transpose(kernels, (0, 2, 3, 1, 4)).reshape(LAYERS, 3 * c, 3 * c)

    pair_map, payload = middle(
        rows, c, group, total_bins, total_band, devices,
        (place, dilation, feats, cot_up, cotangent, cot_down, from_lo, from_hi, offset_embed,
         left_weight, right_weight, taps, back_taps),
    )
    parts = lax.all_to_all(payload, every, 0, 0, tiled=True)
    share, feature_part = pl.pallas_call(
        share_kernel,
        out_shape=(
            jax.ShapeDtypeStruct((devices, 4, HALF), BF16),
            jax.ShapeDtypeStruct((4, HALF), F32),
        ),
        in_specs=[VMEM],
        out_specs=(VMEM,) * 2,
        compiler_params=pltpu.CompilerParams(vmem_limit_bytes=LIMIT),
        name="shares",
    )(parts)
    total = lax.all_to_all(share, every, 0, 0, tiled=True)
    quarters = lax.all_gather(feature_part, "band")
    pairs = quarters.reshape(rows // 2, HALF)
    grad_features = jnp.concatenate([pairs[:, :c], pairs[:, c:]], 0) / math.sqrt(total_band)
    whole_scale = 1.0 / math.sqrt(total_bins * total_band)
    grad_left, grad_right, grad_offset, grad_kernels = pl.pallas_call(
        functools.partial(unpack_kernel, c, whole_scale, 1.0 / math.sqrt(total_bins)),
        out_shape=(
            jax.ShapeDtypeStruct((c, c), F32),
            jax.ShapeDtypeStruct((c, c), F32),
            jax.ShapeDtypeStruct((c, group), F32),
            jax.ShapeDtypeStruct((LAYERS, 3, 3, c, c), F32),
        ),
        in_specs=[SMEM, VMEM],
        out_specs=(VMEM,) * 4,
        compiler_params=pltpu.CompilerParams(vmem_limit_bytes=LIMIT),
        name="unpack",
    )(place, total)
    return pair_map, grad_features, grad_left, grad_right, grad_offset, grad_kernels


def solution(mesh):
    return jax.shard_map(
        per_device,
        mesh=mesh,
        in_specs=(P("bins", None), P(), P(), P(None, "band"), P(), P(), P("bins", None, "band")),
        out_specs=(P("bins", None, "band"), P("bins", None), P(), P(), P(None, "band"), P()),
        check_vma=False,
    )
```

```python
import functools
import math

import jax
import jax.numpy as jnp
from jax import lax
from jax.experimental import pallas as pl
from jax.experimental.pallas import tpu as pltpu
from jax.sharding import PartitionSpec as P

LAYERS = 2
F32 = jnp.float32
BF16 = jnp.bfloat16
HALF = 128
WIDE = 256
RIM0 = 16
RIM1 = 12
RIM2 = 8
RIM3 = 4
CHUNK = 32
LIMIT = 28 * 1024 * 1024
SMALL = 8 * 1024 * 1024
VMEM = pl.BlockSpec(memory_space=pltpu.VMEM)
SMEM = pl.BlockSpec(memory_space=pltpu.SMEM)


def sigmoid(value):
    return 0.5 * jnp.tanh(0.5 * value) + 0.5


def lanes_of(width):
    return lax.broadcasted_iota(jnp.int32, (1, width), 1)


def up(value, amount):
    first = lanes_of(HALF) < amount
    a = pltpu.roll(value[:, :HALF], amount, 1)
    b = pltpu.roll(value[:, HALF:], amount, 1)
    return jnp.concatenate([jnp.where(first, b, a), jnp.where(first, a, b)], 1)


def down(value, amount):
    first = lanes_of(HALF) < HALF - amount
    a = pltpu.roll(value[:, :HALF], HALF - amount, 1)
    b = pltpu.roll(value[:, HALF:], HALF - amount, 1)
    return jnp.concatenate([jnp.where(first, a, b), jnp.where(first, b, a)], 1)


def sweep(count, held, body):
    def step(at, carry):
        for k in range(held):
            body(at * held + k)
        return carry

    lax.fori_loop(0, count // held, step, 0)


def middle_kernel(
    rows, c, total_bins, total_band,
    place, dil, near4, first4, last4, cot_up, cot, cot_down, from_lo, from_hi, emb, lw, rw,
    taps, back_taps, pair_map, payload,
    proj, embed, s0, s1, slope_s, slope0, wide_cot, pairs, g1, g0, sums, edge,
):
    bins = total_bins // rows
    group = emb.shape[1]
    span = group // rows
    first_bin = place[0] * rows
    first_offset = place[1] * group
    rate0, rate1 = dil[0], dil[1]
    edges = from_lo.shape[0] - c

    def rows_at(row, count=1):
        return pl.ds(pl.multiple_of(row * c, c), count * c)

    def mask_of(bin_id):
        lane = lanes_of(WIDE)
        offset = first_offset + jnp.where(lane < 192, lane, lane - WIDE)
        top = jnp.minimum(total_band, total_bins - bin_id)
        top = jnp.where(bin_id >= 0, top, 0)
        return jnp.where((offset >= 0) & (offset < top), 1.0, 0.0).astype(F32)

    def block(blocks, at):
        half = blocks[at * rows // 2 : (at + 1) * rows // 2, :].astype(F32)
        return jnp.concatenate([half[:, :c], half[:, c:]], 0)

    base = place[0] + place[1] * span
    near = [block(near4, k) for k in range(3)]
    window = [block(first4, k) for k in range(4)] + [block(last4, k) for k in range(1, 4)]
    filler = jnp.zeros((WIDE - (span + 3) * rows, c), F32)
    fw = jnp.concatenate(window + [filler], 0).astype(BF16)
    right = jnp.dot(fw, rw[...], preferred_element_type=F32).astype(BF16).astype(F32)
    filler = jnp.zeros((WIDE - 3 * rows, c), F32)
    fl = jnp.concatenate(near + [filler], 0).astype(BF16)
    left = jnp.dot(fl, lw[...], preferred_element_type=F32).astype(BF16).astype(F32)
    proj[...] = jnp.concatenate([right, left], 1).T
    beside = jnp.where(
        lanes_of(HALF) < HALF // 2, from_hi[edges:, :].astype(F32), from_lo[edges:, :].astype(F32)
    )
    embed[...] = jnp.concatenate([emb[...].astype(F32), beside], 1)
    wide_cot[0:RIM2] = cot_up[0 : RIM2 * c, :].reshape(RIM2, c, group)
    wide_cot[RIM2 : RIM2 + rows] = cot[...]
    wide_cot[RIM2 + rows :] = cot_down[0 : RIM2 * c, :].reshape(RIM2, c, group)

    def state_row(row):
        lag = down(proj[0:c, :], RIM0 + row)
        mine = pltpu.roll(proj[c : 2 * c, 0:HALF], HALF - RIM0 - row, 1)[:, 0:1]
        summed = mine + lag + embed[...]
        sig = sigmoid(summed)
        mask = mask_of(first_bin - RIM0 + row)
        s0[rows_at(row), :] = (summed * sig * mask).astype(BF16)
        slope = sig * (1.0 + summed * (1.0 - sig)) * mask
        slope_s[rows_at(row), :] = slope[:, 0:HALF]

    sweep(rows + 2 * RIM0, 16, state_row)

    def convolved(weights, source, base_row, rate):
        view = jnp.concatenate([source[rows_at(base_row + rate * k), :] for k in (-1, 0, 1)], 0)
        parts = jnp.dot(weights, view, preferred_element_type=F32)
        return parts[0:c], parts[c : 2 * c], parts[2 * c : 3 * c]

    def layer_row0(row):
        a, b, d = convolved(taps[0], s0, row + RIM0 - RIM1, rate0)
        pre = up(a, rate0) + b + down(d, rate0)
        sig = sigmoid(pre)
        mask = mask_of(first_bin - RIM1 + row)
        s1[rows_at(row), :] = (pre * sig * mask).astype(BF16)
        slope0[rows_at(row), :] = sig * (1.0 + pre * (1.0 - sig)) * mask

    sweep(rows + 2 * RIM1, 28, layer_row0)

    def layer_row1(row):
        a, b, d = convolved(taps[1], s1, row + RIM1 - RIM2, rate1)
        pre = up(a, rate1) + b + down(d, rate1)
        sig = sigmoid(pre)
        mask = mask_of(first_bin - RIM2 + row)
        slope = sig * (1.0 + pre * (1.0 - sig)) * mask
        pairs[row] = (pre * sig * mask)[:, 0:HALF].astype(BF16)
        tile = rows_at(row // 16)
        turn = (row % 16) * RIM2
        hi = pltpu.roll(from_hi[tile, :].astype(F32), (HALF - turn) % HALF, 1)
        lo = pltpu.roll(from_lo[tile, :].astype(F32), HALF - RIM2 - turn, 1)
        rim = jnp.where(lanes_of(HALF) < HALF // 2, hi, lo)
        grad = jnp.concatenate([wide_cot[row].astype(F32), rim], 1)
        g1[rows_at(row), :] = (grad * slope).astype(BF16)

    sweep(rows + 2 * RIM2, 16, layer_row1)
    pair_map[...] = pairs[RIM2 : RIM2 + rows]

    def back_row(row):
        a, b, d = convolved(back_taps[1], g1, row + RIM2 - RIM3, -rate1)
        back = down(a, rate1) + b + up(d, rate1)
        slope = slope0[rows_at(row + RIM1 - RIM3), :]
        g0[rows_at(row), :] = (back * slope).astype(BF16)

    sweep(rows + 2 * RIM3, 40, back_row)

    def tap_sums(rate, state, rim_s, grads, rim_g):
        lane = lanes_of(HALF)

        def views(row):
            view = [state[rows_at(row + rim_s + rate * k), :] for k in (-1, 0, 1)]
            grad = grads[rows_at(row + rim_g), 0:HALF].astype(F32)
            low = pltpu.roll(grad, HALF - rate, 1)
            high = pltpu.roll(grad, rate, 1)
            low0 = jnp.where(lane < HALF - rate, low, 0.0)
            high1 = jnp.where(lane < rate, high, 0.0)
            first = jnp.concatenate([low0, grad, high - high1], 0)
            second = jnp.concatenate([low - low0, jnp.zeros_like(grad), high1], 0)
            return jnp.concatenate(view, 0), jnp.concatenate([first, second], 1).astype(BF16)

        def step(at, total):
            both = [views(at * CHUNK + k) for k in range(CHUNK)]
            view = jnp.concatenate([v for v, _ in both], 1)
            grad = jnp.concatenate([g for _, g in both], 1)
            return total + lax.dot_general(
                view, grad, (((1,), (1,)), ((), ())), preferred_element_type=F32
            )

        return lax.fori_loop(0, rows // CHUNK, step, jnp.zeros((3 * c, 3 * c), F32))

    def place_rows(start, value):
        count = value.shape[0] // 4
        payload[start // 4 : start // 4 + count, 4:8, :] = value.reshape(count, 4, HALF).astype(
            BF16
        )

    total1 = tap_sums(rate1, s1, RIM1, g1, RIM2)
    place_rows(3 * c, total1[:, 0:HALF])
    edge[...] = total1[:, HALF : 3 * c]
    total0 = tap_sums(rate0, s0, RIM0, g0, RIM3)
    place_rows(0, total0[:, 0:HALF])
    place_rows(6 * c, jnp.concatenate([total0[:, HALF : 3 * c], edge[...]], 1))

    sums[...] = jnp.zeros_like(sums)
    lane = lanes_of(HALF)

    def last_row(row):
        a, b, d = convolved(back_taps[0], g0, row + RIM3, -rate0)
        back = (down(a, rate0) + b + up(d, rate0))[:, 0:HALF]
        grad = back * slope_s[rows_at(row + RIM0), :]
        total = jnp.sum(grad, axis=1, keepdims=True)
        sums[:, 0:HALF] += jnp.where(lane == row, total, 0.0)
        turned = pltpu.roll(grad, row, 1)
        wrapped = jnp.where(lane < row, turned, 0.0)
        sums[:, HALF : 2 * HALF] += turned - wrapped
        sums[:, 2 * HALF : 3 * HALF] += wrapped
        sums[:, 3 * HALF : 4 * HALF] += grad

    sweep(rows, 16, last_row)

    highest = lax.Precision.HIGHEST
    both = sums[:, 0 : 3 * HALF]
    both = jnp.concatenate([both, jnp.zeros_like(both)], 0).T
    left_grad = both[0:rows, 0:c]
    right_grad = both[HALF : HALF + rows + group, 0:c]
    fwin = jnp.concatenate([near[1]] + window[1 : span + 2], 0)
    fwin = jnp.concatenate([fwin, jnp.zeros((WIDE - fwin.shape[0], c), F32)], 0)
    fwin = jnp.concatenate([fwin, jnp.zeros_like(fwin)], 1).T[0:c]
    grad_left = jnp.dot(fwin[:, 0:rows], left_grad, precision=highest, preferred_element_type=F32)
    grad_right = jnp.dot(
        fwin[:, rows : 2 * rows + group], right_grad, precision=highest, preferred_element_type=F32
    )
    place_rows(9 * c, jnp.concatenate([grad_left, grad_right], 1))
    spare = payload.shape[0] - 10 * c // 4
    payload[10 * c // 4 :, 4:8, :] = jnp.zeros((spare, 4, HALF), BF16)
    at = pl.ds((10 * c + place[1] * c) // 4, c // 4)
    payload[at, 4:8, :] = sums[:, 3 * HALF : 4 * HALF].reshape(c // 4, 4, HALF).astype(BF16)

    transposed = (((1,), (1,)), ((), ()))
    feature_left = lax.dot_general(
        left_grad, lw[...].astype(F32), transposed, precision=highest, preferred_element_type=F32
    )
    feature_right = lax.dot_general(
        right_grad, rw[...].astype(F32), transposed, precision=highest, preferred_element_type=F32
    )
    payload[:, 0:4, :] = jnp.zeros((payload.shape[0], 4, HALF), BF16)

    def packed(value):
        return jnp.concatenate([value[0 : rows // 2], value[rows // 2 :]], 1).reshape(4, 4, HALF)

    mine = pl.ds(place[0] * 4, 4)
    payload[mine, 0:4, :] = packed(feature_left).astype(BF16)
    for k in range(span + 1):
        part = packed(feature_right[k * rows : (k + 1) * rows])

        @pl.when(base + k < bins)
        def _():
            target = pl.ds((base + k) * 4, 4)
            old = payload[target, 0:4, :].astype(F32)
            payload[target, 0:4, :] = (old + part).astype(BF16)


def middle(rows, c, group, total_bins, total_band, devices, args):
    tall = lambda rim: (rows + 2 * rim) * c
    return pl.pallas_call(
        functools.partial(middle_kernel, rows, c, total_bins, total_band),
        out_shape=(
            jax.ShapeDtypeStruct((rows, c, group), BF16),
            jax.ShapeDtypeStruct((devices, 8, HALF), BF16),
        ),
        in_specs=[SMEM] * 2 + [VMEM] * (len(args) - 2),
        out_specs=(VMEM,) * 2,
        scratch_shapes=[
            pltpu.VMEM((2 * c, WIDE), F32),
            pltpu.VMEM((c, WIDE), F32),
            pltpu.VMEM((tall(RIM0), WIDE), BF16),
            pltpu.VMEM((tall(RIM1), WIDE), BF16),
            pltpu.VMEM((tall(RIM0), HALF), F32),
            pltpu.VMEM((tall(RIM1), WIDE), F32),
            pltpu.VMEM((rows + 2 * RIM2, c, HALF), BF16),
            pltpu.VMEM((rows + 2 * RIM2, c, HALF), BF16),
            pltpu.VMEM((tall(RIM2), WIDE), BF16),
            pltpu.VMEM((tall(RIM3), WIDE), BF16),
            pltpu.VMEM((c, 4 * HALF), F32),
            pltpu.VMEM((3 * c, 3 * c - HALF), F32),
        ],
        compiler_params=pltpu.CompilerParams(vmem_limit_bytes=LIMIT),
        name="middle",
    )(*args)


def edge_kernel(rows, c, cot_up, cot, cot_down, own, beyond, emb, to_lo, to_hi, blocks):
    lane = lanes_of(HALF)
    count = rows + 2 * RIM2
    for tile in range(count // 16):
        low = jnp.zeros((c, HALF), F32)
        high = jnp.zeros((c, HALF), F32)
        for k in range(16):
            row = tile * 16 + k
            if row < RIM2:
                value = cot_up[row * c : (row + 1) * c, :]
            elif row < RIM2 + rows:
                value = cot[row - RIM2]
            else:
                value = cot_down[(row - RIM2 - rows) * c : (row - RIM2 - rows + 1) * c, :]
            value = value.astype(F32)
            here = (lane >= RIM2 * k) & (lane < RIM2 * (k + 1))
            low = jnp.where(here, pltpu.roll(value, RIM2 * k, 1), low)
            high = jnp.where(here, pltpu.roll(value, RIM2 * (k + 1) % HALF, 1), high)
        to_lo[tile * c : (tile + 1) * c, :] = low.astype(BF16)
        to_hi[tile * c : (tile + 1) * c, :] = high.astype(BF16)
    to_lo[count // 16 * c :, :] = emb[...]
    to_hi[count // 16 * c :, :] = emb[...]
    half = rows // 2
    blocks[0:half, :] = cot_up[RIM2 * c :, :]
    blocks[half : 2 * half, :] = own[...]
    blocks[2 * half : 3 * half, :] = cot_down[RIM2 * c :, :]
    blocks[3 * half :, :] = beyond[...]


def greet_kernel(rows, c, features, first, last, to_up, to_down, own):
    half = rows // 2
    packed = jnp.concatenate([features[0:half, :], features[half:, :]], 1)
    own[...] = packed
    to_down[0 : RIM2 * c, :] = first[...].reshape(RIM2 * c, HALF)
    to_down[RIM2 * c :, :] = packed
    to_up[0 : RIM2 * c, :] = last[...].reshape(RIM2 * c, HALF)
    to_up[RIM2 * c :, :] = packed


def unpack_kernel(c, whole_scale, offset_scale, place, total, left, right, offset, kernels):
    def piece(start):
        value = total[start // 4 : (start + c) // 4].astype(F32)
        return value.reshape(c, HALF)

    for p in range(3):
        rest = piece((6 + p) * c) * whole_scale
        for layer in range(2):
            main = piece((3 * layer + p) * c) * whole_scale
            kernels[layer, p, 0] = main[:, 0:c]
            kernels[layer, p, 1] = main[:, c : 2 * c]
            kernels[layer, p, 2] = rest[:, layer * c : (layer + 1) * c]
    both = piece(9 * c) * whole_scale
    left[...] = both[:, 0:c]
    right[...] = both[:, c : 2 * c]
    at = pl.ds((10 * c + place[1] * c) // 4, c // 4)
    offset[...] = total[at].astype(F32).reshape(c, HALF) * offset_scale


def per_device(features, left_weight, right_weight, offset_embed, kernels, dilation, cotangent):
    rows, c = features.shape
    group = offset_embed.shape[1]
    bins, band = lax.axis_size("bins"), lax.axis_size("band")
    devices = bins * band
    total_bins, total_band = rows * bins, group * band
    every = ("bins", "band")
    place = jnp.stack([lax.axis_index("bins"), lax.axis_index("band")]).astype(jnp.int32)

    def beside(block, axis, step):
        count = lax.axis_size(axis)
        route = [(i + step, i) for i in range(count) if 0 <= i + step < count]
        return lax.ppermute(block, axis, route)

    def joint(block, step):
        route = []
        for i in range(bins):
            for b in range(band):
                source = i + b * (group // rows) + step
                if source < bins:
                    route.append((source * band + b, i * band + b))
        return lax.ppermute(block, every, route)

    half = rows // 2
    greeting = jax.ShapeDtypeStruct((RIM2 * c + half, HALF), BF16)
    block_of = jax.ShapeDtypeStruct((half, HALF), BF16)
    last = rows // RIM2 - 1
    to_up, to_down, own = pl.pallas_call(
        functools.partial(greet_kernel, rows, c),
        grid=(1,),
        out_shape=(greeting, greeting, block_of),
        in_specs=[
            pl.BlockSpec((rows, c), lambda _: (0, 0)),
            pl.BlockSpec((RIM2, c, group), lambda _: (0, 0, 0)),
            pl.BlockSpec((RIM2, c, group), lambda _: (last, 0, 0)),
        ],
        out_specs=(
            pl.BlockSpec(greeting.shape, lambda _: (0, 0)),
            pl.BlockSpec(greeting.shape, lambda _: (0, 0)),
            pl.BlockSpec(block_of.shape, lambda _: (0, 0)),
        ),
        compiler_params=pltpu.CompilerParams(vmem_limit_bytes=SMALL),
        name="greet",
    )(features, cotangent, cotangent)
    cot_up = beside(to_up, "bins", -1)
    cot_down = beside(to_down, "bins", 1)
    beyond = beside(own, "bins", 2)
    edge_shape = jax.ShapeDtypeStruct(((rows + 2 * RIM2) // 16 * c + c, HALF), BF16)
    to_lo, to_hi, blocks = pl.pallas_call(
        functools.partial(edge_kernel, rows, c),
        out_shape=(edge_shape, edge_shape, jax.ShapeDtypeStruct((4 * half, HALF), BF16)),
        in_specs=[VMEM] * 6,
        out_specs=(VMEM,) * 3,
        compiler_params=pltpu.CompilerParams(vmem_limit_bytes=SMALL),
        name="edges",
    )(cot_up, cotangent, cot_down, own, beyond, offset_embed)
    first4 = joint(blocks, 0)
    last4 = joint(blocks, 3)
    from_lo = beside(to_hi, "band", -1)
    from_hi = beside(to_lo, "band", 1)

    taps = jnp.transpose(kernels, (0, 2, 4, 1, 3)).reshape(LAYERS, 3 * c, 3 * c)
    back_taps = jnp.transpose(kernels, (0, 2, 3, 1, 4)).reshape(LAYERS, 3 * c, 3 * c)

    pair_map, payload = middle(
        rows, c, group, total_bins, total_band, devices,
        (place, dilation, blocks, first4, last4, cot_up, cotangent, cot_down, from_lo, from_hi,
         offset_embed, left_weight, right_weight, taps, back_taps),
    )
    parts = lax.all_to_all(payload, every, 0, 0, tiled=True)
    summed = jnp.sum(parts.astype(F32), axis=0)
    feature_part = summed[:4]
    share = jnp.broadcast_to(summed[None, 4:].astype(BF16), (devices, 4, HALF))
    total = lax.all_to_all(share, every, 0, 0, tiled=True)
    quarters = lax.all_gather(feature_part, "band")
    pairs = quarters.reshape(rows // 2, HALF)
    grad_features = jnp.concatenate([pairs[:, :c], pairs[:, c:]], 0) / math.sqrt(total_band)
    whole_scale = 1.0 / math.sqrt(total_bins * total_band)
    grad_left, grad_right, grad_offset, grad_kernels = pl.pallas_call(
        functools.partial(unpack_kernel, c, whole_scale, 1.0 / math.sqrt(total_bins)),
        out_shape=(
            jax.ShapeDtypeStruct((c, c), F32),
            jax.ShapeDtypeStruct((c, c), F32),
            jax.ShapeDtypeStruct((c, group), F32),
            jax.ShapeDtypeStruct((LAYERS, 3, 3, c, c), F32),
        ),
        in_specs=[SMEM, VMEM],
        out_specs=(VMEM,) * 4,
        compiler_params=pltpu.CompilerParams(vmem_limit_bytes=SMALL),
        name="unpack",
    )(place, total)
    return pair_map, grad_features, grad_left, grad_right, grad_offset, grad_kernels


def solution(mesh):
    return jax.shard_map(
        per_device,
        mesh=mesh,
        in_specs=(P("bins", None), P(), P(), P(None, "band"), P(), P(), P("bins", None, "band")),
        out_specs=(P("bins", None, "band"), P("bins", None), P(), P(), P(None, "band"), P()),
        check_vma=False,
    )
```

```python
import functools
import math

import jax
import jax.numpy as jnp
from jax import lax
from jax.experimental import pallas as pl
from jax.experimental.pallas import tpu as pltpu
from jax.sharding import PartitionSpec as P

LAYERS = 2
F32 = jnp.float32
BF16 = jnp.bfloat16
HALF = 128
WIDE = 256
RIM0 = 16
RIM1 = 12
RIM2 = 8
RIM3 = 4
CHUNK = 32
HELD = 32
LIMIT = 28 * 1024 * 1024
SMALL = 8 * 1024 * 1024
VMEM = pl.BlockSpec(memory_space=pltpu.VMEM)
SMEM = pl.BlockSpec(memory_space=pltpu.SMEM)


def sigmoid(value):
    return 0.5 * jnp.tanh(0.5 * value) + 0.5


def lanes_of(width):
    return lax.broadcasted_iota(jnp.int32, (1, width), 1)


def up(value, amount):
    first = lanes_of(HALF) < amount
    a = pltpu.roll(value[:, :HALF], amount, 1)
    b = pltpu.roll(value[:, HALF:], amount, 1)
    return jnp.concatenate([jnp.where(first, b, a), jnp.where(first, a, b)], 1)


def down(value, amount):
    first = lanes_of(HALF) < HALF - amount
    a = pltpu.roll(value[:, :HALF], HALF - amount, 1)
    b = pltpu.roll(value[:, HALF:], HALF - amount, 1)
    return jnp.concatenate([jnp.where(first, a, b), jnp.where(first, b, a)], 1)


def sweep(count, held, body, before=None):
    def step(at, carry):
        given = () if before is None else before(at)
        for k in range(held):
            body(at * held + k, k, *given)
        return carry

    lax.fori_loop(0, count // held, step, 0)


def lane_sums(values):
    lane = lanes_of(HALF)
    span = 1
    while len(values) > 1:
        even = (lane // span) % 2 == 0
        values = [
            jnp.where(even, a, b) + pltpu.roll(jnp.where(even, b, a), HALF - span, 1)
            for a, b in zip(values[0::2], values[1::2])
        ]
        span *= 2
    (total,) = values
    while span < HALF:
        total = total + pltpu.roll(total, span, 1)
        span *= 2
    return total


def middle_kernel(
    rows, c, total_bins, total_band,
    place, dil, feats, cot_up, cot, cot_down, from_lo, from_hi, emb, lw, rw, taps, back_taps,
    pair_map, payload,
    proj, lefts, pick, embed, s0, s1, slope_s, slope0, wide_cot, pairs, g1, g0, sums, edge,
):
    bins = total_bins // rows
    group = emb.shape[1]
    span = group // rows
    first_bin = place[0] * rows
    first_offset = place[1] * group
    rate0, rate1 = dil[0], dil[1]
    edges = from_lo.shape[0] - c

    def rows_at(row, count=1):
        return pl.ds(pl.multiple_of(row * c, c), count * c)

    def mask_of(bin_id):
        lane = lanes_of(WIDE)
        offset = first_offset + jnp.where(lane < 192, lane, lane - WIDE)
        top = jnp.minimum(total_band, total_bins - bin_id)
        top = jnp.where(bin_id >= 0, top, 0)
        return jnp.where((offset >= 0) & (offset < top), 1.0, 0.0).astype(F32)

    def block(index):
        half = feats[jnp.clip(index, 0, bins - 1)].astype(F32)
        return jnp.concatenate([half[:, :c], half[:, c:]], 0)

    base = place[0] + place[1] * span
    near = [block(place[0] + k) for k in (-1, 0, 1)]
    window = [block(base + k) for k in range(-1, span + 2)]
    filler = jnp.zeros((WIDE - (span + 3) * rows, c), F32)
    fw = jnp.concatenate(window + [filler], 0).astype(BF16)
    right = jnp.dot(fw, rw[...], preferred_element_type=F32).astype(BF16).astype(F32)
    proj[...] = jnp.concatenate([right, jnp.zeros_like(right)], 1).T[0:c]
    fl = jnp.concatenate(near, 0).astype(BF16)
    lefts[...] = jnp.dot(fl, lw[...], preferred_element_type=F32).astype(BF16)
    lane = lax.broadcasted_iota(jnp.int32, (16, 16 * HALF), 1)
    which = lax.broadcasted_iota(jnp.int32, (16, 16 * HALF), 0)
    pick[...] = jnp.where(lane // HALF == which, 1.0, 0.0).astype(BF16)
    beside = jnp.where(
        lanes_of(HALF) < HALF // 2, from_hi[edges:, :].astype(F32), from_lo[edges:, :].astype(F32)
    )
    embed[...] = jnp.concatenate([emb[...].astype(F32), beside], 1)
    wide_cot[0:RIM2] = cot_up[...]
    wide_cot[RIM2 : RIM2 + rows] = cot[...]
    wide_cot[RIM2 + rows :] = cot_down[...]

    def state_step(at):
        mine = lax.dot_general(
            lefts[pl.ds(pl.multiple_of(at * 16 + RIM0, 16), 16), :], pick[...],
            (((0,), (0,)), ((), ())), preferred_element_type=F32,
        )
        return (mine,)

    def state_row(row, k, mine):
        lag = down(proj[...], RIM0 + row)
        mine = mine[:, k * HALF : (k + 1) * HALF]
        summed = jnp.concatenate([mine, mine], 1) + lag + embed[...]
        sig = sigmoid(summed)
        mask = mask_of(first_bin - RIM0 + row)
        s0[rows_at(row), :] = (summed * sig * mask).astype(BF16)
        slope = sig * (1.0 + summed * (1.0 - sig)) * mask
        slope_s[rows_at(row), :] = slope[:, 0:HALF]

    sweep(rows + 2 * RIM0, 16, state_row, state_step)

    def convolved(weights, source, base_row, rate):
        view = jnp.concatenate([source[rows_at(base_row + rate * k), :] for k in (-1, 0, 1)], 0)
        parts = jnp.dot(weights, view, preferred_element_type=F32)
        return parts[0:c], parts[c : 2 * c], parts[2 * c : 3 * c]

    def layer_row0(row, k):
        a, b, d = convolved(taps[0], s0, row + RIM0 - RIM1, rate0)
        pre = up(a, rate0) + b + down(d, rate0)
        sig = sigmoid(pre)
        mask = mask_of(first_bin - RIM1 + row)
        s1[rows_at(row), :] = (pre * sig * mask).astype(BF16)
        slope0[rows_at(row), :] = sig * (1.0 + pre * (1.0 - sig)) * mask

    sweep(rows + 2 * RIM1, 56, layer_row0)

    def layer_step1(at):
        return from_lo[rows_at(at), :].astype(F32), from_hi[rows_at(at), :].astype(F32)

    def layer_row1(row, k, lo, hi):
        a, b, d = convolved(taps[1], s1, row + RIM1 - RIM2, rate1)
        pre = up(a, rate1) + b + down(d, rate1)
        sig = sigmoid(pre)
        mask = mask_of(first_bin - RIM2 + row)
        slope = sig * (1.0 + pre * (1.0 - sig)) * mask
        pairs[row] = (pre * sig * mask)[:, 0:HALF].astype(BF16)
        lo = pltpu.roll(lo, (HALF - RIM2 * (k + 1)) % HALF, 1)
        hi = pltpu.roll(hi, (HALF - RIM2 * k) % HALF, 1)
        rim = jnp.where(lanes_of(HALF) < HALF // 2, hi, lo)
        grad = jnp.concatenate([wide_cot[row].astype(F32), rim], 1)
        g1[rows_at(row), :] = (grad * slope).astype(BF16)

    sweep(rows + 2 * RIM2, 16, layer_row1, layer_step1)
    pair_map[...] = pairs[RIM2 : RIM2 + rows]

    def back_row(row, k):
        a, b, d = convolved(back_taps[1], g1, row + RIM2 - RIM3, -rate1)
        back = down(a, rate1) + b + up(d, rate1)
        slope = slope0[rows_at(row + RIM1 - RIM3), :]
        g0[rows_at(row), :] = (back * slope).astype(BF16)

    sweep(rows + 2 * RIM3, 40, back_row)

    def tap_sums(rate, state, rim_s, grads, rim_g):
        lane = lanes_of(HALF)

        def views(row):
            view = [state[rows_at(row + rim_s + rate * k), :] for k in (-1, 0, 1)]
            grad = grads[rows_at(row + rim_g), 0:HALF].astype(F32)
            low = pltpu.roll(grad, HALF - rate, 1)
            high = pltpu.roll(grad, rate, 1)
            low0 = jnp.where(lane < HALF - rate, low, 0.0)
            high1 = jnp.where(lane < rate, high, 0.0)
            first = jnp.concatenate([low0, grad, high - high1], 0)
            second = jnp.concatenate([low - low0, jnp.zeros_like(grad), high1], 0)
            return jnp.concatenate(view, 0), jnp.concatenate([first, second], 1).astype(BF16)

        def step(at, total):
            both = [views(at * CHUNK + k) for k in range(CHUNK)]
            view = jnp.concatenate([v for v, _ in both], 1)
            grad = jnp.concatenate([g for _, g in both], 1)
            return total + lax.dot_general(
                view, grad, (((1,), (1,)), ((), ())), preferred_element_type=F32
            )

        return lax.fori_loop(0, rows // CHUNK, step, jnp.zeros((3 * c, 3 * c), F32))

    def place_rows(start, value):
        count = value.shape[0] // 4
        payload[start // 4 : start // 4 + count, 4:8, :] = value.reshape(count, 4, HALF).astype(
            BF16
        )

    total1 = tap_sums(rate1, s1, RIM1, g1, RIM2)
    place_rows(3 * c, total1[:, 0:HALF])
    edge[...] = total1[:, HALF : 3 * c]
    total0 = tap_sums(rate0, s0, RIM0, g0, RIM3)
    place_rows(0, total0[:, 0:HALF])
    place_rows(6 * c, jnp.concatenate([total0[:, HALF : 3 * c], edge[...]], 1))

    sums[...] = jnp.zeros_like(sums)
    lane = lanes_of(HALF)

    def last_step(at, carry):
        grads = []
        offset_sum = jnp.zeros((c, HALF), F32)
        window = jnp.zeros((c, HALF), F32)
        wrap = jnp.zeros((c, HALF), F32)
        for k in range(HELD):
            row = at * HELD + k
            a, b, d = convolved(back_taps[0], g0, row + RIM3, -rate0)
            back = (down(a, rate0) + b + up(d, rate0))[:, 0:HALF]
            grad = back * slope_s[rows_at(row + RIM0), :]
            grads.append(grad)
            offset_sum = offset_sum + grad
            turned = pltpu.roll(grad, k, 1) if k else grad
            wrapped = jnp.where(lane < k, turned, 0.0)
            window = window + (turned - wrapped)
            wrap = wrap + wrapped
        here = (lane >= at * HELD) & (lane < (at + 1) * HELD)
        sums[:, 0:HALF] += jnp.where(here, lane_sums(grads), 0.0)
        first = lane < at * HELD
        window = pltpu.roll(window, at * HELD, 1)
        wrap = pltpu.roll(wrap, at * HELD, 1)
        sums[:, HALF : 2 * HALF] += jnp.where(first, 0.0, window)
        sums[:, 2 * HALF : 3 * HALF] += jnp.where(first, window, 0.0) + wrap
        sums[:, 3 * HALF : 4 * HALF] += offset_sum
        return carry

    lax.fori_loop(0, rows // HELD, last_step, 0)

    highest = lax.Precision.HIGHEST
    both = sums[:, 0 : 3 * HALF]
    both = jnp.concatenate([both, jnp.zeros_like(both)], 0).T
    left_grad = both[0:rows, 0:c]
    right_grad = both[HALF : HALF + rows + group, 0:c]
    fwin = jnp.concatenate([near[1]] + window[1 : span + 2], 0)
    fwin = jnp.concatenate([fwin, jnp.zeros((WIDE - fwin.shape[0], c), F32)], 0)
    fwin = jnp.concatenate([fwin, jnp.zeros_like(fwin)], 1).T[0:c]
    grad_left = jnp.dot(fwin[:, 0:rows], left_grad, precision=highest, preferred_element_type=F32)
    grad_right = jnp.dot(
        fwin[:, rows : 2 * rows + group], right_grad, precision=highest, preferred_element_type=F32
    )
    place_rows(9 * c, jnp.concatenate([grad_left, grad_right], 1))
    spare = payload.shape[0] - 10 * c // 4
    payload[10 * c // 4 :, 4:8, :] = jnp.zeros((spare, 4, HALF), BF16)
    at = pl.ds((10 * c + place[1] * c) // 4, c // 4)
    payload[at, 4:8, :] = sums[:, 3 * HALF : 4 * HALF].reshape(c // 4, 4, HALF).astype(BF16)

    transposed = (((1,), (1,)), ((), ()))
    feature_left = lax.dot_general(
        left_grad, lw[...].astype(F32), transposed, precision=highest, preferred_element_type=F32
    )
    feature_right = lax.dot_general(
        right_grad, rw[...].astype(F32), transposed, precision=highest, preferred_element_type=F32
    )
    payload[:, 0:4, :] = jnp.zeros((payload.shape[0], 4, HALF), BF16)

    def packed(value):
        return jnp.concatenate([value[0 : rows // 2], value[rows // 2 :]], 1).reshape(4, 4, HALF)

    mine = pl.ds(place[0] * 4, 4)
    payload[mine, 0:4, :] = packed(feature_left).astype(BF16)
    for k in range(span + 1):
        part = packed(feature_right[k * rows : (k + 1) * rows])

        @pl.when(base + k < bins)
        def _():
            target = pl.ds((base + k) * 4, 4)
            old = payload[target, 0:4, :].astype(F32)
            payload[target, 0:4, :] = (old + part).astype(BF16)


def middle(rows, c, group, total_bins, total_band, devices, args):
    tall = lambda rim: (rows + 2 * rim) * c
    return pl.pallas_call(
        functools.partial(middle_kernel, rows, c, total_bins, total_band),
        out_shape=(
            jax.ShapeDtypeStruct((rows, c, group), BF16),
            jax.ShapeDtypeStruct((devices, 8, HALF), BF16),
        ),
        in_specs=[SMEM] * 2 + [VMEM] * (len(args) - 2),
        out_specs=(VMEM,) * 2,
        scratch_shapes=[
            pltpu.VMEM((c, WIDE), F32),
            pltpu.VMEM((3 * rows, c), BF16),
            pltpu.VMEM((16, 16 * HALF), BF16),
            pltpu.VMEM((c, WIDE), F32),
            pltpu.VMEM((tall(RIM0), WIDE), BF16),
            pltpu.VMEM((tall(RIM1), WIDE), BF16),
            pltpu.VMEM((tall(RIM0), HALF), F32),
            pltpu.VMEM((tall(RIM1), WIDE), F32),
            pltpu.VMEM((rows + 2 * RIM2, c, HALF), BF16),
            pltpu.VMEM((rows + 2 * RIM2, c, HALF), BF16),
            pltpu.VMEM((tall(RIM2), WIDE), BF16),
            pltpu.VMEM((tall(RIM3), WIDE), BF16),
            pltpu.VMEM((c, 4 * HALF), F32),
            pltpu.VMEM((3 * c, 3 * c - HALF), F32),
        ],
        compiler_params=pltpu.CompilerParams(vmem_limit_bytes=LIMIT),
        name="middle",
    )(*args)


def edge_kernel(rows, c, cot_up, cot, cot_down, emb, to_lo, to_hi):
    lane = lanes_of(HALF)
    count = rows + 2 * RIM2
    for tile in range(count // 16):
        low = jnp.zeros((c, HALF), F32)
        high = jnp.zeros((c, HALF), F32)
        for k in range(16):
            row = tile * 16 + k
            if row < RIM2:
                value = cot_up[row]
            elif row < RIM2 + rows:
                value = cot[row - RIM2]
            else:
                value = cot_down[row - RIM2 - rows]
            value = value.astype(F32)
            here = (lane >= RIM2 * k) & (lane < RIM2 * (k + 1))
            low = jnp.where(here, pltpu.roll(value, RIM2 * k, 1), low)
            high = jnp.where(here, pltpu.roll(value, RIM2 * (k + 1) % HALF, 1), high)
        to_lo[tile * c : (tile + 1) * c, :] = low.astype(BF16)
        to_hi[tile * c : (tile + 1) * c, :] = high.astype(BF16)
    to_lo[count // 16 * c :, :] = emb[...]
    to_hi[count // 16 * c :, :] = emb[...]


def greet_kernel(rows, c, features, everywhere):
    packed = jnp.concatenate([features[0 : rows // 2, :], features[rows // 2 :, :]], 1)
    everywhere[...] = jnp.broadcast_to(packed[None], everywhere.shape)


def unpack_kernel(c, whole_scale, offset_scale, place, total, left, right, offset, kernels):
    def piece(start):
        value = total[start // 4 : (start + c) // 4].astype(F32)
        return value.reshape(c, HALF)

    for p in range(3):
        rest = piece((6 + p) * c) * whole_scale
        for layer in range(2):
            main = piece((3 * layer + p) * c) * whole_scale
            kernels[layer, p, 0] = main[:, 0:c]
            kernels[layer, p, 1] = main[:, c : 2 * c]
            kernels[layer, p, 2] = rest[:, layer * c : (layer + 1) * c]
    both = piece(9 * c) * whole_scale
    left[...] = both[:, 0:c]
    right[...] = both[:, c : 2 * c]
    at = pl.ds((10 * c + place[1] * c) // 4, c // 4)
    offset[...] = total[at].astype(F32).reshape(c, HALF) * offset_scale


def per_device(features, left_weight, right_weight, offset_embed, kernels, dilation, cotangent):
    rows, c = features.shape
    group = offset_embed.shape[1]
    bins, band = lax.axis_size("bins"), lax.axis_size("band")
    devices = bins * band
    total_bins, total_band = rows * bins, group * band
    every = ("bins", "band")
    place = jnp.stack([lax.axis_index("bins"), lax.axis_index("band")]).astype(jnp.int32)

    def beside(block, axis, step):
        count = lax.axis_size(axis)
        return lax.ppermute(block, axis, [((i + step) % count, i) for i in range(count)])

    everywhere = pl.pallas_call(
        functools.partial(greet_kernel, rows, c),
        out_shape=jax.ShapeDtypeStruct((bins, rows // 2, HALF), BF16),
        in_specs=[VMEM],
        out_specs=VMEM,
        compiler_params=pltpu.CompilerParams(vmem_limit_bytes=SMALL),
        name="greet",
    )(features)
    feats = lax.all_to_all(everywhere, "bins", 0, 0, tiled=True)
    cot_up = beside(cotangent[rows - RIM2 :], "bins", -1)
    cot_down = beside(cotangent[:RIM2], "bins", 1)
    edge_shape = jax.ShapeDtypeStruct(((rows + 2 * RIM2) // 16 * c + c, HALF), BF16)
    to_lo, to_hi = pl.pallas_call(
        functools.partial(edge_kernel, rows, c),
        out_shape=(edge_shape, edge_shape),
        in_specs=[VMEM] * 4,
        out_specs=(VMEM,) * 2,
        compiler_params=pltpu.CompilerParams(vmem_limit_bytes=SMALL),
        name="edges",
    )(cot_up, cotangent, cot_down, offset_embed)
    from_lo = beside(to_hi, "band", -1)
    from_hi = beside(to_lo, "band", 1)

    taps = jnp.transpose(kernels, (0, 2, 4, 1, 3)).reshape(LAYERS, 3 * c, 3 * c)
    back_taps = jnp.transpose(kernels, (0, 2, 3, 1, 4)).reshape(LAYERS, 3 * c, 3 * c)

    pair_map, payload = middle(
        rows, c, group, total_bins, total_band, devices,
        (place, dilation, feats, cot_up, cotangent, cot_down, from_lo, from_hi, offset_embed,
         left_weight, right_weight, taps, back_taps),
    )
    parts = lax.all_to_all(payload, every, 0, 0, tiled=True)
    summed = jnp.sum(parts.astype(F32), axis=0)
    feature_part = summed[:4]
    share = jnp.broadcast_to(summed[None, 4:].astype(BF16), (devices, 4, HALF))
    total = lax.all_to_all(share, every, 0, 0, tiled=True)
    quarters = lax.all_gather(feature_part, "band")
    pairs = quarters.reshape(rows // 2, HALF)
    grad_features = jnp.concatenate([pairs[:, :c], pairs[:, c:]], 0) / math.sqrt(total_band)
    whole_scale = 1.0 / math.sqrt(total_bins * total_band)
    grad_left, grad_right, grad_offset, grad_kernels = pl.pallas_call(
        functools.partial(unpack_kernel, c, whole_scale, 1.0 / math.sqrt(total_bins)),
        out_shape=(
            jax.ShapeDtypeStruct((c, c), F32),
            jax.ShapeDtypeStruct((c, c), F32),
            jax.ShapeDtypeStruct((c, group), F32),
            jax.ShapeDtypeStruct((LAYERS, 3, 3, c, c), F32),
        ),
        in_specs=[SMEM, VMEM],
        out_specs=(VMEM,) * 4,
        compiler_params=pltpu.CompilerParams(vmem_limit_bytes=SMALL),
        name="unpack",
    )(place, total)
    return pair_map, grad_features, grad_left, grad_right, grad_offset, grad_kernels


def solution(mesh):
    return jax.shard_map(
        per_device,
        mesh=mesh,
        in_specs=(P("bins", None), P(), P(), P(None, "band"), P(), P(), P("bins", None, "band")),
        out_specs=(P("bins", None, "band"), P("bins", None), P(), P(), P(None, "band"), P()),
        check_vma=False,
    )
```

```python
import functools
import math

import jax
import jax.numpy as jnp
from jax import lax
from jax.experimental import pallas as pl
from jax.experimental.pallas import tpu as pltpu
from jax.sharding import PartitionSpec as P

LAYERS = 2
F32 = jnp.float32
BF16 = jnp.bfloat16
HALF = 128
WIDE = 256
RIM0 = 16
RIM1 = 12
RIM2 = 8
RIM3 = 4
CHUNK = 32
HELD0 = 64
HELD = 32
LIMIT = 28 * 1024 * 1024
SMALL = 8 * 1024 * 1024
WHOLE = 56 * 1024 * 1024
VMEM = pl.BlockSpec(memory_space=pltpu.VMEM)
SMEM = pl.BlockSpec(memory_space=pltpu.SMEM)


def sigmoid(value):
    return 0.5 * jnp.tanh(0.5 * value) + 0.5


def lanes_of(width):
    return lax.broadcasted_iota(jnp.int32, (1, width), 1)


def up(value, amount):
    first = lanes_of(HALF) < amount
    a = pltpu.roll(value[:, :HALF], amount, 1)
    b = pltpu.roll(value[:, HALF:], amount, 1)
    return jnp.concatenate([jnp.where(first, b, a), jnp.where(first, a, b)], 1)


def down(value, amount):
    first = lanes_of(HALF) < HALF - amount
    a = pltpu.roll(value[:, :HALF], HALF - amount, 1)
    b = pltpu.roll(value[:, HALF:], HALF - amount, 1)
    return jnp.concatenate([jnp.where(first, a, b), jnp.where(first, b, a)], 1)


def sweep(count, held, body, before=None):
    def step(at, carry):
        given = () if before is None else before(at)
        for k in range(held):
            body(at * held + k, k, *given)
        return carry

    if held == count:
        step(0, 0)
    else:
        lax.fori_loop(0, count // held, step, 0)


def lane_sums(values):
    lane = lanes_of(HALF)
    span = 1
    while len(values) > 1:
        even = (lane // span) % 2 == 0
        values = [
            jnp.where(even, a, b) + pltpu.roll(jnp.where(even, b, a), HALF - span, 1)
            for a, b in zip(values[0::2], values[1::2])
        ]
        span *= 2
    (total,) = values
    while span < HALF:
        total = total + pltpu.roll(total, span, 1)
        span *= 2
    return total


def middle_kernel(
    rows, c, total_bins, total_band,
    place, dil, feats, cot_up, cot, cot_down, from_lo, from_hi, emb, lw, rw, taps, back_taps,
    pair_map, payload,
    proj, lefts, pick, embed, s0, s1, slope_s, slope0, wide_cot, pairs, g1, g0, sums, edge,
):
    bins = total_bins // rows
    group = emb.shape[1]
    span = group // rows
    first_bin = place[0] * rows
    first_offset = place[1] * group
    rate0, rate1 = dil[0], dil[1]
    edges = from_lo.shape[0] - c

    def rows_at(row, count=1):
        start = row * c
        return pl.ds(start if isinstance(row, int) else pl.multiple_of(start, c), count * c)

    def rows_of(start, count):
        return pl.ds(start if isinstance(start, int) else pl.multiple_of(start, 16), count)

    def mask_of(bin_id):
        lane = lanes_of(WIDE)
        offset = first_offset + jnp.where(lane < 192, lane, lane - WIDE)
        top = jnp.minimum(total_band, total_bins - bin_id)
        top = jnp.where(bin_id >= 0, top, 0)
        return jnp.where((offset >= 0) & (offset < top), 1.0, 0.0).astype(F32)

    def block(index):
        half = feats[jnp.clip(index, 0, bins - 1)].astype(F32)
        return jnp.concatenate([half[:, :c], half[:, c:]], 0)

    base = place[0] + place[1] * span
    near = [block(place[0] + k) for k in (-1, 0, 1)]
    window = [block(base + k) for k in range(-1, span + 2)]
    filler = jnp.zeros((WIDE - (span + 3) * rows, c), F32)
    fw = jnp.concatenate(window + [filler], 0).astype(BF16)
    right = jnp.dot(fw, rw[...], preferred_element_type=F32).astype(BF16).astype(F32)
    proj[...] = jnp.concatenate([right, jnp.zeros_like(right)], 1).T[0:c]
    fl = jnp.concatenate(near, 0).astype(BF16)
    lefts[...] = jnp.dot(fl, lw[...], preferred_element_type=F32).astype(BF16)
    lane = lax.broadcasted_iota(jnp.int32, (HELD0, HELD0 * HALF), 1)
    which = lax.broadcasted_iota(jnp.int32, (HELD0, HELD0 * HALF), 0)
    pick[...] = jnp.where(lane // HALF == which, 1.0, 0.0).astype(BF16)
    beside = jnp.where(
        lanes_of(HALF) < HALF // 2, from_hi[edges:, :].astype(F32), from_lo[edges:, :].astype(F32)
    )
    embed[...] = jnp.concatenate([emb[...].astype(F32), beside], 1)
    wide_cot[0:RIM2] = cot_up[...]
    wide_cot[RIM2 : RIM2 + rows] = cot[...]
    wide_cot[RIM2 + rows :] = cot_down[...]

    def state_step(at):
        mine = lax.dot_general(
            lefts[rows_of(at * HELD0 + RIM0, HELD0), :], pick[...],
            (((0,), (0,)), ((), ())), preferred_element_type=F32,
        )
        return (mine,)

    def state_row(row, k, mine):
        lag = down(proj[...], RIM0 + row)
        mine = mine[:, k * HALF : (k + 1) * HALF]
        summed = jnp.concatenate([mine, mine], 1) + lag + embed[...]
        sig = sigmoid(summed)
        mask = mask_of(first_bin - RIM0 + row)
        s0[rows_at(row), :] = (summed * sig * mask).astype(BF16)
        slope = sig * (1.0 + summed * (1.0 - sig)) * mask
        slope_s[rows_at(row), :] = slope[:, 0:HALF]

    sweep(rows + 2 * RIM0, HELD0, state_row, state_step)

    def convolved(weights, source, base_row, rate):
        view = jnp.concatenate([source[rows_at(base_row + rate * k), :] for k in (-1, 0, 1)], 0)
        parts = jnp.dot(weights, view, preferred_element_type=F32)
        return parts[0:c], parts[c : 2 * c], parts[2 * c : 3 * c]

    def layer_row0(row, k):
        a, b, d = convolved(taps[0], s0, row + RIM0 - RIM1, rate0)
        pre = up(a, rate0) + b + down(d, rate0)
        sig = sigmoid(pre)
        mask = mask_of(first_bin - RIM1 + row)
        s1[rows_at(row), :] = (pre * sig * mask).astype(BF16)
        slope0[rows_at(row), :] = sig * (1.0 + pre * (1.0 - sig)) * mask

    sweep(rows + 2 * RIM1, 56, layer_row0)

    def layer_step1(at):
        tiles = [rows_at(tile) for tile in range((rows + 2 * RIM2) // 16)]
        return [(from_lo[t, :].astype(F32), from_hi[t, :].astype(F32)) for t in tiles]

    def layer_row1(row, k, *tiles):
        a, b, d = convolved(taps[1], s1, row + RIM1 - RIM2, rate1)
        pre = up(a, rate1) + b + down(d, rate1)
        sig = sigmoid(pre)
        mask = mask_of(first_bin - RIM2 + row)
        slope = sig * (1.0 + pre * (1.0 - sig)) * mask
        pairs[row] = (pre * sig * mask)[:, 0:HALF].astype(BF16)
        lo, hi = tiles[k // 16]
        here = lanes_of(HALF) // RIM2 == k % 16
        rim = pltpu.roll(jnp.where(here, hi, lo), (HALF - RIM2 * (k % 16)) % HALF, 1)
        grad = jnp.concatenate([wide_cot[row].astype(F32), rim], 1)
        g1[rows_at(row), :] = (grad * slope).astype(BF16)

    sweep(rows + 2 * RIM2, rows + 2 * RIM2, layer_row1, layer_step1)
    pair_map[...] = pairs[RIM2 : RIM2 + rows]

    def back_row(row, k):
        a, b, d = convolved(back_taps[1], g1, row + RIM2 - RIM3, -rate1)
        back = down(a, rate1) + b + up(d, rate1)
        slope = slope0[rows_at(row + RIM1 - RIM3), :]
        g0[rows_at(row), :] = (back * slope).astype(BF16)

    sweep(rows + 2 * RIM3, 40, back_row)

    def tap_sums(rate, state, rim_s, grads, rim_g):
        lane = lanes_of(HALF)

        def views(row):
            view = [state[rows_at(row + rim_s + rate * k), :] for k in (-1, 0, 1)]
            grad = grads[rows_at(row + rim_g), 0:HALF].astype(F32)
            low = pltpu.roll(grad, HALF - rate, 1)
            high = pltpu.roll(grad, rate, 1)
            low0 = jnp.where(lane < HALF - rate, low, 0.0)
            high1 = jnp.where(lane < rate, high, 0.0)
            first = jnp.concatenate([low0, grad, high - high1], 0)
            second = jnp.concatenate([low - low0, jnp.zeros_like(grad), high1], 0)
            return jnp.concatenate(view, 0), jnp.concatenate([first, second], 1).astype(BF16)

        def step(at, total):
            both = [views(at * CHUNK + k) for k in range(CHUNK)]
            view = jnp.concatenate([v for v, _ in both], 1)
            grad = jnp.concatenate([g for _, g in both], 1)
            return total + lax.dot_general(
                view, grad, (((1,), (1,)), ((), ())), preferred_element_type=F32
            )

        return lax.fori_loop(0, rows // CHUNK, step, jnp.zeros((3 * c, 3 * c), F32))

    def place_rows(start, value):
        count = value.shape[0] // 4
        payload[start // 4 : start // 4 + count, 4:8, :] = value.reshape(count, 4, HALF).astype(
            BF16
        )

    total1 = tap_sums(rate1, s1, RIM1, g1, RIM2)
    place_rows(3 * c, total1[:, 0:HALF])
    edge[...] = total1[:, HALF : 3 * c]
    total0 = tap_sums(rate0, s0, RIM0, g0, RIM3)
    place_rows(0, total0[:, 0:HALF])
    place_rows(6 * c, jnp.concatenate([total0[:, HALF : 3 * c], edge[...]], 1))

    sums[...] = jnp.zeros_like(sums)
    lane = lanes_of(HALF)

    def last_step(at, carry):
        grads = []
        offset_sum = jnp.zeros((c, HALF), F32)
        window = jnp.zeros((c, HALF), F32)
        wrap = jnp.zeros((c, HALF), F32)
        for k in range(HELD):
            row = at * HELD + k
            a, b, d = convolved(back_taps[0], g0, row + RIM3, -rate0)
            back = (down(a, rate0) + b + up(d, rate0))[:, 0:HALF]
            grad = back * slope_s[rows_at(row + RIM0), :]
            grads.append(grad)
            offset_sum = offset_sum + grad
            turned = pltpu.roll(grad, k, 1) if k else grad
            wrapped = jnp.where(lane < k, turned, 0.0)
            window = window + (turned - wrapped)
            wrap = wrap + wrapped
        here = (lane >= at * HELD) & (lane < (at + 1) * HELD)
        sums[:, 0:HALF] += jnp.where(here, lane_sums(grads), 0.0)
        first = lane < at * HELD
        window = pltpu.roll(window, at * HELD, 1)
        wrap = pltpu.roll(wrap, at * HELD, 1)
        sums[:, HALF : 2 * HALF] += jnp.where(first, 0.0, window)
        sums[:, 2 * HALF : 3 * HALF] += jnp.where(first, window, 0.0) + wrap
        sums[:, 3 * HALF : 4 * HALF] += offset_sum
        return carry

    if rows == HELD:
        last_step(0, 0)
    else:
        lax.fori_loop(0, rows // HELD, last_step, 0)

    highest = lax.Precision.HIGHEST
    both = sums[:, 0 : 3 * HALF]
    both = jnp.concatenate([both, jnp.zeros_like(both)], 0).T
    left_grad = both[0:rows, 0:c]
    right_grad = both[HALF : HALF + rows + group, 0:c]
    fwin = jnp.concatenate([near[1]] + window[1 : span + 2], 0)
    fwin = jnp.concatenate([fwin, jnp.zeros((WIDE - fwin.shape[0], c), F32)], 0)
    fwin = jnp.concatenate([fwin, jnp.zeros_like(fwin)], 1).T[0:c]
    grad_left = jnp.dot(fwin[:, 0:rows], left_grad, precision=highest, preferred_element_type=F32)
    grad_right = jnp.dot(
        fwin[:, rows : 2 * rows + group], right_grad, precision=highest, preferred_element_type=F32
    )
    place_rows(9 * c, jnp.concatenate([grad_left, grad_right], 1))
    spare = payload.shape[0] - 10 * c // 4
    payload[10 * c // 4 :, 4:8, :] = jnp.zeros((spare, 4, HALF), BF16)
    at = pl.ds((10 * c + place[1] * c) // 4, c // 4)
    payload[at, 4:8, :] = sums[:, 3 * HALF : 4 * HALF].reshape(c // 4, 4, HALF).astype(BF16)

    transposed = (((1,), (1,)), ((), ()))
    feature_left = lax.dot_general(
        left_grad, lw[...].astype(F32), transposed, precision=highest, preferred_element_type=F32
    )
    feature_right = lax.dot_general(
        right_grad, rw[...].astype(F32), transposed, precision=highest, preferred_element_type=F32
    )
    payload[:, 0:4, :] = jnp.zeros((payload.shape[0], 4, HALF), BF16)

    def packed(value):
        return jnp.concatenate([value[0 : rows // 2], value[rows // 2 :]], 1).reshape(4, 4, HALF)

    mine = pl.ds(place[0] * 4, 4)
    payload[mine, 0:4, :] = packed(feature_left).astype(BF16)
    for k in range(span + 1):
        part = packed(feature_right[k * rows : (k + 1) * rows])

        @pl.when(base + k < bins)
        def _():
            target = pl.ds((base + k) * 4, 4)
            old = payload[target, 0:4, :].astype(F32)
            payload[target, 0:4, :] = (old + part).astype(BF16)


def middle(rows, c, group, total_bins, total_band, devices, args):
    tall = lambda rim: (rows + 2 * rim) * c
    return pl.pallas_call(
        functools.partial(middle_kernel, rows, c, total_bins, total_band),
        out_shape=(
            jax.ShapeDtypeStruct((rows, c, group), BF16),
            jax.ShapeDtypeStruct((devices, 8, HALF), BF16),
        ),
        in_specs=[SMEM] * 2 + [VMEM] * (len(args) - 2),
        out_specs=(VMEM,) * 2,
        scratch_shapes=[
            pltpu.VMEM((c, WIDE), F32),
            pltpu.VMEM((3 * rows, c), BF16),
            pltpu.VMEM((HELD0, HELD0 * HALF), BF16),
            pltpu.VMEM((c, WIDE), F32),
            pltpu.VMEM((tall(RIM0), WIDE), BF16),
            pltpu.VMEM((tall(RIM1), WIDE), BF16),
            pltpu.VMEM((tall(RIM0), HALF), F32),
            pltpu.VMEM((tall(RIM1), WIDE), F32),
            pltpu.VMEM((rows + 2 * RIM2, c, HALF), BF16),
            pltpu.VMEM((rows + 2 * RIM2, c, HALF), BF16),
            pltpu.VMEM((tall(RIM2), WIDE), BF16),
            pltpu.VMEM((tall(RIM3), WIDE), BF16),
            pltpu.VMEM((c, 4 * HALF), F32),
            pltpu.VMEM((3 * c, 3 * c - HALF), F32),
        ],
        compiler_params=pltpu.CompilerParams(vmem_limit_bytes=LIMIT),
        name="middle",
    )(*args)


def edge_kernel(rows, c, cot_up, cot, cot_down, emb, to_lo, to_hi):
    lane = lanes_of(HALF)
    count = rows + 2 * RIM2
    for tile in range(count // 16):
        low = jnp.zeros((c, HALF), F32)
        high = jnp.zeros((c, HALF), F32)
        for k in range(16):
            row = tile * 16 + k
            if row < RIM2:
                value = cot_up[row]
            elif row < RIM2 + rows:
                value = cot[row - RIM2]
            else:
                value = cot_down[row - RIM2 - rows]
            value = value.astype(F32)
            value = pltpu.roll(value, RIM2 * k, 1)
            low = jnp.where(lane // RIM2 == k, value, low)
            high = jnp.where(lane // RIM2 == (k + 15) % 16, value, high)
        to_lo[tile * c : (tile + 1) * c, :] = low.astype(BF16)
        to_hi[tile * c : (tile + 1) * c, :] = high.astype(BF16)
    to_lo[count // 16 * c :, :] = emb[...]
    to_hi[count // 16 * c :, :] = emb[...]


def greet_kernel(rows, features, first, last, everywhere, low, high):
    low[...] = first[...]
    high[...] = last[...]
    packed = jnp.concatenate([features[0 : rows // 2, :], features[rows // 2 :, :]], 1)
    everywhere[...] = jnp.broadcast_to(packed[None], everywhere.shape)


def unpack_kernel(c, whole_scale, offset_scale, place, total, left, right, offset, kernels):
    def piece(start):
        value = total[start // 4 : (start + c) // 4].astype(F32)
        return value.reshape(c, HALF)

    for p in range(3):
        rest = piece((6 + p) * c) * whole_scale
        for layer in range(2):
            main = piece((3 * layer + p) * c) * whole_scale
            kernels[layer, p, 0] = main[:, 0:c]
            kernels[layer, p, 1] = main[:, c : 2 * c]
            kernels[layer, p, 2] = rest[:, layer * c : (layer + 1) * c]
    both = piece(9 * c) * whole_scale
    left[...] = both[:, 0:c]
    right[...] = both[:, c : 2 * c]
    at = pl.ds((10 * c + place[1] * c) // 4, c // 4)
    offset[...] = total[at].astype(F32).reshape(c, HALF) * offset_scale


def per_device(features, left_weight, right_weight, offset_embed, kernels, dilation, cotangent):
    rows, c = features.shape
    group = offset_embed.shape[1]
    bins, band = lax.axis_size("bins"), lax.axis_size("band")
    devices = bins * band
    total_bins, total_band = rows * bins, group * band
    every = ("bins", "band")
    place = jnp.stack([lax.axis_index("bins"), lax.axis_index("band")]).astype(jnp.int32)

    def beside(block, axis, step):
        count = lax.axis_size(axis)
        return lax.ppermute(block, axis, [((i + step) % count, i) for i in range(count)])

    end = rows // RIM2 - 1
    row_block = (RIM2, c, group)
    everywhere, low, high = pl.pallas_call(
        functools.partial(greet_kernel, rows),
        grid=(1,),
        out_shape=(
            jax.ShapeDtypeStruct((bins, rows // 2, HALF), BF16),
            jax.ShapeDtypeStruct(row_block, BF16),
            jax.ShapeDtypeStruct(row_block, BF16),
        ),
        in_specs=[
            pl.BlockSpec((rows, c), lambda _: (0, 0)),
            pl.BlockSpec(row_block, lambda _: (0, 0, 0)),
            pl.BlockSpec(row_block, lambda _: (end, 0, 0)),
        ],
        out_specs=(
            pl.BlockSpec((bins, rows // 2, HALF), lambda _: (0, 0, 0)),
            pl.BlockSpec(row_block, lambda _: (0, 0, 0)),
            pl.BlockSpec(row_block, lambda _: (0, 0, 0)),
        ),
        compiler_params=pltpu.CompilerParams(vmem_limit_bytes=WHOLE),
        name="greet",
    )(features, cotangent, cotangent)
    feats = lax.all_to_all(everywhere, "bins", 0, 0, tiled=True)
    cot_up, cot_down = beside(high, "bins", -1), beside(low, "bins", 1)
    edge_shape = jax.ShapeDtypeStruct(((rows + 2 * RIM2) // 16 * c + c, HALF), BF16)
    to_lo, to_hi = pl.pallas_call(
        functools.partial(edge_kernel, rows, c),
        out_shape=(edge_shape, edge_shape),
        in_specs=[VMEM] * 4,
        out_specs=(VMEM,) * 2,
        compiler_params=pltpu.CompilerParams(vmem_limit_bytes=SMALL),
        name="edges",
    )(cot_up, cotangent, cot_down, offset_embed)
    from_lo = beside(to_hi, "band", -1)
    from_hi = beside(to_lo, "band", 1)

    taps = jnp.transpose(kernels, (0, 2, 4, 1, 3)).reshape(LAYERS, 3 * c, 3 * c)
    back_taps = jnp.transpose(kernels, (0, 2, 3, 1, 4)).reshape(LAYERS, 3 * c, 3 * c)

    pair_map, payload = middle(
        rows, c, group, total_bins, total_band, devices,
        (place, dilation, feats, cot_up, cotangent, cot_down, from_lo, from_hi, offset_embed,
         left_weight, right_weight, taps, back_taps),
    )
    parts = lax.all_to_all(payload, every, 0, 0, tiled=True)
    summed = jnp.sum(parts.astype(F32), axis=0)
    feature_part = summed[:4]
    share = jnp.broadcast_to(summed[None, 4:].astype(BF16), (devices, 4, HALF))
    total = lax.all_to_all(share, every, 0, 0, tiled=True)
    quarters = lax.all_gather(feature_part, "band")
    pairs = quarters.reshape(rows // 2, HALF)
    grad_features = jnp.concatenate([pairs[:, :c], pairs[:, c:]], 0) / math.sqrt(total_band)
    whole_scale = 1.0 / math.sqrt(total_bins * total_band)
    grad_left, grad_right, grad_offset, grad_kernels = pl.pallas_call(
        functools.partial(unpack_kernel, c, whole_scale, 1.0 / math.sqrt(total_bins)),
        out_shape=(
            jax.ShapeDtypeStruct((c, c), F32),
            jax.ShapeDtypeStruct((c, c), F32),
            jax.ShapeDtypeStruct((c, group), F32),
            jax.ShapeDtypeStruct((LAYERS, 3, 3, c, c), F32),
        ),
        in_specs=[SMEM, VMEM],
        out_specs=(VMEM,) * 4,
        compiler_params=pltpu.CompilerParams(vmem_limit_bytes=SMALL),
        name="unpack",
    )(place, total)
    return pair_map, grad_features, grad_left, grad_right, grad_offset, grad_kernels


def solution(mesh):
    return jax.shard_map(
        per_device,
        mesh=mesh,
        in_specs=(P("bins", None), P(), P(), P(None, "band"), P(), P(), P("bins", None, "band")),
        out_specs=(P("bins", None, "band"), P("bins", None), P(), P(), P(None, "band"), P()),
        check_vma=False,
    )
```

```python
import functools
import math

import jax
import jax.numpy as jnp
from jax import lax
from jax.experimental import pallas as pl
from jax.experimental.pallas import tpu as pltpu
from jax.sharding import PartitionSpec as P

LAYERS = 2
F32 = jnp.float32
BF16 = jnp.bfloat16
HALF = 128
WIDE = 256
RIM0 = 16
RIM1 = 12
RIM2 = 8
RIM3 = 4
CHUNK = 32
HELD0 = 64
HELD = 32
LIMIT = 28 * 1024 * 1024
SMALL = 8 * 1024 * 1024
WHOLE = 56 * 1024 * 1024
VMEM = pl.BlockSpec(memory_space=pltpu.VMEM)
SMEM = pl.BlockSpec(memory_space=pltpu.SMEM)


def sigmoid(value):
    return 0.5 * jnp.tanh(0.5 * value) + 0.5


def lanes_of(width):
    return lax.broadcasted_iota(jnp.int32, (1, width), 1)


def up(value, amount):
    first = lanes_of(HALF) < amount
    a = pltpu.roll(value[:, :HALF], amount, 1)
    b = pltpu.roll(value[:, HALF:], amount, 1)
    return jnp.concatenate([jnp.where(first, b, a), jnp.where(first, a, b)], 1)


def down(value, amount):
    first = lanes_of(HALF) < HALF - amount
    a = pltpu.roll(value[:, :HALF], HALF - amount, 1)
    b = pltpu.roll(value[:, HALF:], HALF - amount, 1)
    return jnp.concatenate([jnp.where(first, a, b), jnp.where(first, b, a)], 1)


def sweep(count, held, body, before=None):
    def step(at, carry):
        given = () if before is None else before(at)
        for k in range(held):
            body(at * held + k, k, *given)
        return carry

    if held == count:
        step(0, 0)
    else:
        lax.fori_loop(0, count // held, step, 0)


def lane_sums(values):
    lane = lanes_of(HALF)
    span = 1
    while len(values) > 1:
        even = (lane // span) % 2 == 0
        values = [
            jnp.where(even, a, b) + pltpu.roll(jnp.where(even, b, a), HALF - span, 1)
            for a, b in zip(values[0::2], values[1::2])
        ]
        span *= 2
    (total,) = values
    while span < HALF:
        total = total + pltpu.roll(total, span, 1)
        span *= 2
    return total


def middle_kernel(
    rows, c, total_bins, total_band,
    place, dil, feats, cot_up, cot, cot_down, from_lo, from_hi, emb, lw, rw, taps, back_taps,
    pair_map, payload,
    proj, lefts, pick, embed, s0, s1, slope_s, slope0, wide_cot, pairs, g1, g0, sums, edge,
):
    bins = total_bins // rows
    group = emb.shape[1]
    span = group // rows
    first_bin = place[0] * rows
    first_offset = place[1] * group
    rate0, rate1 = dil[0], dil[1]
    edges = from_lo.shape[0] - c

    def rows_at(row, count=1):
        start = row * c
        return pl.ds(start if isinstance(row, int) else pl.multiple_of(start, c), count * c)

    def rows_of(start, count):
        return pl.ds(start if isinstance(start, int) else pl.multiple_of(start, 16), count)

    def mask_of(bin_id):
        lane = lanes_of(WIDE)
        offset = first_offset + jnp.where(lane < 192, lane, lane - WIDE)
        top = jnp.minimum(total_band, total_bins - bin_id)
        top = jnp.where(bin_id >= 0, top, 0)
        return jnp.where((offset >= 0) & (offset < top), 1.0, 0.0).astype(F32)

    def block(index):
        half = feats[jnp.clip(index, 0, bins - 1)].astype(F32)
        return jnp.concatenate([half[:, :c], half[:, c:]], 0)

    base = place[0] + place[1] * span
    near = [block(place[0] + k) for k in (-1, 0, 1)]
    window = [block(base + k) for k in range(-1, span + 2)]
    filler = jnp.zeros((WIDE - (span + 3) * rows, c), F32)
    fw = jnp.concatenate(window + [filler], 0).astype(BF16)
    right = jnp.dot(fw, rw[...], preferred_element_type=F32).astype(BF16).astype(F32)
    proj[...] = jnp.concatenate([right, jnp.zeros_like(right)], 1).T[0:c]
    fl = jnp.concatenate(near, 0).astype(BF16)
    lefts[...] = jnp.dot(fl, lw[...], preferred_element_type=F32).astype(BF16)
    lane = lax.broadcasted_iota(jnp.int32, (HELD0, HELD0 * HALF), 1)
    which = lax.broadcasted_iota(jnp.int32, (HELD0, HELD0 * HALF), 0)
    pick[...] = jnp.where(lane // HALF == which, 1.0, 0.0).astype(BF16)
    beside = jnp.where(
        lanes_of(HALF) < HALF // 2, from_hi[edges:, :].astype(F32), from_lo[edges:, :].astype(F32)
    )
    embed[...] = jnp.concatenate([emb[...].astype(F32), beside], 1)
    wide_cot[0:RIM2] = cot_up[...]
    wide_cot[RIM2 : RIM2 + rows] = cot[...]
    wide_cot[RIM2 + rows :] = cot_down[...]

    def state_step(at):
        mine = lax.dot_general(
            lefts[rows_of(at * HELD0 + RIM0, HELD0), :], pick[...],
            (((0,), (0,)), ((), ())), preferred_element_type=F32,
        )
        return (mine,)

    def state_row(row, k, mine):
        lag = down(proj[...], RIM0 + row)
        mine = mine[:, k * HALF : (k + 1) * HALF]
        summed = jnp.concatenate([mine, mine], 1) + lag + embed[...]
        sig = sigmoid(summed)
        mask = mask_of(first_bin - RIM0 + row)
        s0[rows_at(row), :] = (summed * sig * mask).astype(BF16)
        slope = sig * (1.0 + summed * (1.0 - sig)) * mask
        slope_s[rows_at(row), :] = slope[:, 0:HALF]

    sweep(rows + 2 * RIM0, HELD0, state_row, state_step)

    def convolved(weights, source, base_row, rate):
        view = jnp.concatenate([source[rows_at(base_row + rate * k), :] for k in (-1, 0, 1)], 0)
        parts = jnp.dot(weights, view, preferred_element_type=F32)
        return parts[0:c], parts[c : 2 * c], parts[2 * c : 3 * c]

    def layer_row0(row, k):
        a, b, d = convolved(taps[0], s0, row + RIM0 - RIM1, rate0)
        pre = up(a, rate0) + b + down(d, rate0)
        sig = sigmoid(pre)
        mask = mask_of(first_bin - RIM1 + row)
        s1[rows_at(row), :] = (pre * sig * mask).astype(BF16)
        slope0[rows_at(row), :] = sig * (1.0 + pre * (1.0 - sig)) * mask

    sweep(rows + 2 * RIM1, 56, layer_row0)

    def layer_step1(at):
        tiles = [rows_at(tile) for tile in range((rows + 2 * RIM2) // 16)]
        return [(from_lo[t, :].astype(F32), from_hi[t, :].astype(F32)) for t in tiles]

    def layer_row1(row, k, *tiles):
        a, b, d = convolved(taps[1], s1, row + RIM1 - RIM2, rate1)
        pre = up(a, rate1) + b + down(d, rate1)
        sig = sigmoid(pre)
        mask = mask_of(first_bin - RIM2 + row)
        slope = sig * (1.0 + pre * (1.0 - sig)) * mask
        pairs[row] = (pre * sig * mask)[:, 0:HALF].astype(BF16)
        lo, hi = tiles[k // 16]
        here = lanes_of(HALF) // RIM2 == k % 16
        rim = pltpu.roll(jnp.where(here, hi, lo), (HALF - RIM2 * (k % 16)) % HALF, 1)
        grad = jnp.concatenate([wide_cot[row].astype(F32), rim], 1)
        g1[rows_at(row), :] = (grad * slope).astype(BF16)

    sweep(rows + 2 * RIM2, rows + 2 * RIM2, layer_row1, layer_step1)
    pair_map[...] = pairs[RIM2 : RIM2 + rows]

    def back_row(row, k):
        a, b, d = convolved(back_taps[1], g1, row + RIM2 - RIM3, -rate1)
        back = down(a, rate1) + b + up(d, rate1)
        slope = slope0[rows_at(row + RIM1 - RIM3), :]
        g0[rows_at(row), :] = (back * slope).astype(BF16)

    sweep(rows + 2 * RIM3, 40, back_row)

    def tap_sums(rate, state, rim_s, grads, rim_g):
        lane = lanes_of(HALF)

        def views(row):
            view = [state[rows_at(row + rim_s + rate * k), :] for k in (-1, 0, 1)]
            grad = grads[rows_at(row + rim_g), 0:HALF].astype(F32)
            low = pltpu.roll(grad, HALF - rate, 1)
            high = pltpu.roll(grad, rate, 1)
            low0 = jnp.where(lane < HALF - rate, low, 0.0)
            high1 = jnp.where(lane < rate, high, 0.0)
            first = jnp.concatenate([low0, grad, high - high1], 0)
            second = jnp.concatenate([low - low0, jnp.zeros_like(grad), high1], 0)
            return jnp.concatenate(view, 0), jnp.concatenate([first, second], 1).astype(BF16)

        def step(at, total):
            both = [views(at * CHUNK + k) for k in range(CHUNK)]
            view = jnp.concatenate([v for v, _ in both], 1)
            grad = jnp.concatenate([g for _, g in both], 1)
            return total + lax.dot_general(
                view, grad, (((1,), (1,)), ((), ())), preferred_element_type=F32
            )

        return lax.fori_loop(0, rows // CHUNK, step, jnp.zeros((3 * c, 3 * c), F32))

    def place_rows(start, value):
        count = value.shape[0] // 4
        payload[start // 4 : start // 4 + count, 4:8, :] = value.reshape(count, 4, HALF).astype(
            BF16
        )

    total1 = tap_sums(rate1, s1, RIM1, g1, RIM2)
    place_rows(3 * c, total1[:, 0:HALF])
    edge[...] = total1[:, HALF : 3 * c]
    total0 = tap_sums(rate0, s0, RIM0, g0, RIM3)
    place_rows(0, total0[:, 0:HALF])
    place_rows(6 * c, jnp.concatenate([total0[:, HALF : 3 * c], edge[...]], 1))

    sums[...] = jnp.zeros_like(sums)
    lane = lanes_of(HALF)

    def last_step(at, carry):
        grads = []
        offset_sum = jnp.zeros((c, HALF), F32)
        window = jnp.zeros((c, HALF), F32)
        wrap = jnp.zeros((c, HALF), F32)
        for k in range(HELD):
            row = at * HELD + k
            a, b, d = convolved(back_taps[0], g0, row + RIM3, -rate0)
            back = (down(a, rate0) + b + up(d, rate0))[:, 0:HALF]
            grad = back * slope_s[rows_at(row + RIM0), :]
            grads.append(grad)
            offset_sum = offset_sum + grad
            turned = pltpu.roll(grad, k, 1) if k else grad
            wrapped = jnp.where(lane < k, turned, 0.0)
            window = window + turned
            wrap = wrap + wrapped
        window = window - wrap
        here = (lane >= at * HELD) & (lane < (at + 1) * HELD)
        sums[:, 0:HALF] += jnp.where(here, lane_sums(grads), 0.0)
        first = lane < at * HELD
        window = pltpu.roll(window, at * HELD, 1)
        wrap = pltpu.roll(wrap, at * HELD, 1)
        sums[:, HALF : 2 * HALF] += jnp.where(first, 0.0, window)
        sums[:, 2 * HALF : 3 * HALF] += jnp.where(first, window, 0.0) + wrap
        sums[:, 3 * HALF : 4 * HALF] += offset_sum
        return carry

    if rows == HELD:
        last_step(0, 0)
    else:
        lax.fori_loop(0, rows // HELD, last_step, 0)

    highest = lax.Precision.HIGHEST
    both = sums[:, 0 : 3 * HALF]
    both = jnp.concatenate([both, jnp.zeros_like(both)], 0).T
    left_grad = both[0:rows, 0:c]
    right_grad = both[HALF : HALF + rows + group, 0:c]
    fwin = jnp.concatenate([near[1]] + window[1 : span + 2], 0)
    fwin = jnp.concatenate([fwin, jnp.zeros((WIDE - fwin.shape[0], c), F32)], 0)
    fwin = jnp.concatenate([fwin, jnp.zeros_like(fwin)], 1).T[0:c]
    grad_left = jnp.dot(fwin[:, 0:rows], left_grad, precision=highest, preferred_element_type=F32)
    grad_right = jnp.dot(
        fwin[:, rows : 2 * rows + group], right_grad, precision=highest, preferred_element_type=F32
    )
    place_rows(9 * c, jnp.concatenate([grad_left, grad_right], 1))
    spare = payload.shape[0] - 10 * c // 4
    payload[10 * c // 4 :, 4:8, :] = jnp.zeros((spare, 4, HALF), BF16)
    at = pl.ds((10 * c + place[1] * c) // 4, c // 4)
    payload[at, 4:8, :] = sums[:, 3 * HALF : 4 * HALF].reshape(c // 4, 4, HALF).astype(BF16)

    transposed = (((1,), (1,)), ((), ()))
    feature_left = lax.dot_general(
        left_grad, lw[...].astype(F32), transposed, precision=highest, preferred_element_type=F32
    )
    feature_right = lax.dot_general(
        right_grad, rw[...].astype(F32), transposed, precision=highest, preferred_element_type=F32
    )
    payload[:, 0:4, :] = jnp.zeros((payload.shape[0], 4, HALF), BF16)

    def packed(value):
        return jnp.concatenate([value[0 : rows // 2], value[rows // 2 :]], 1).reshape(4, 4, HALF)

    mine = pl.ds(place[0] * 4, 4)
    payload[mine, 0:4, :] = packed(feature_left).astype(BF16)
    for k in range(span + 1):
        part = packed(feature_right[k * rows : (k + 1) * rows])

        @pl.when(base + k < bins)
        def _():
            target = pl.ds((base + k) * 4, 4)
            old = payload[target, 0:4, :].astype(F32)
            payload[target, 0:4, :] = (old + part).astype(BF16)


def middle(rows, c, group, total_bins, total_band, devices, args):
    tall = lambda rim: (rows + 2 * rim) * c
    return pl.pallas_call(
        functools.partial(middle_kernel, rows, c, total_bins, total_band),
        out_shape=(
            jax.ShapeDtypeStruct((rows, c, group), BF16),
            jax.ShapeDtypeStruct((devices, 8, HALF), BF16),
        ),
        in_specs=[SMEM] * 2 + [VMEM] * (len(args) - 2),
        out_specs=(VMEM,) * 2,
        scratch_shapes=[
            pltpu.VMEM((c, WIDE), F32),
            pltpu.VMEM((3 * rows, c), BF16),
            pltpu.VMEM((HELD0, HELD0 * HALF), BF16),
            pltpu.VMEM((c, WIDE), F32),
            pltpu.VMEM((tall(RIM0), WIDE), BF16),
            pltpu.VMEM((tall(RIM1), WIDE), BF16),
            pltpu.VMEM((tall(RIM0), HALF), F32),
            pltpu.VMEM((tall(RIM1), WIDE), F32),
            pltpu.VMEM((rows + 2 * RIM2, c, HALF), BF16),
            pltpu.VMEM((rows + 2 * RIM2, c, HALF), BF16),
            pltpu.VMEM((tall(RIM2), WIDE), BF16),
            pltpu.VMEM((tall(RIM3), WIDE), BF16),
            pltpu.VMEM((c, 4 * HALF), F32),
            pltpu.VMEM((3 * c, 3 * c - HALF), F32),
        ],
        compiler_params=pltpu.CompilerParams(vmem_limit_bytes=LIMIT),
        name="middle",
    )(*args)


def edge_kernel(rows, c, cot_up, cot, cot_down, emb, to_lo, to_hi):
    lane = lanes_of(HALF)
    count = rows + 2 * RIM2
    for tile in range(count // 16):
        low = jnp.zeros((c, HALF), F32)
        high = jnp.zeros((c, HALF), F32)
        for k in range(16):
            row = tile * 16 + k
            if row < RIM2:
                value = cot_up[row]
            elif row < RIM2 + rows:
                value = cot[row - RIM2]
            else:
                value = cot_down[row - RIM2 - rows]
            value = value.astype(F32)
            value = pltpu.roll(value, RIM2 * k, 1)
            low = jnp.where(lane // RIM2 == k, value, low)
            high = jnp.where(lane // RIM2 == (k + 15) % 16, value, high)
        to_lo[tile * c : (tile + 1) * c, :] = low.astype(BF16)
        to_hi[tile * c : (tile + 1) * c, :] = high.astype(BF16)
    to_lo[count // 16 * c :, :] = emb[...]
    to_hi[count // 16 * c :, :] = emb[...]


def greet_kernel(rows, features, first, last, everywhere, low, high):
    low[...] = first[...]
    high[...] = last[...]
    packed = jnp.concatenate([features[0 : rows // 2, :], features[rows // 2 :, :]], 1)
    everywhere[...] = jnp.broadcast_to(packed[None], everywhere.shape)


def unpack_kernel(c, whole_scale, offset_scale, place, total, left, right, offset, kernels):
    def piece(start):
        return total[start : start + c, :].astype(F32)

    for p in range(3):
        rest = piece((6 + p) * c) * whole_scale
        for layer in range(2):
            main = piece((3 * layer + p) * c) * whole_scale
            kernels[layer, p, 0] = main[:, 0:c]
            kernels[layer, p, 1] = main[:, c : 2 * c]
            kernels[layer, p, 2] = rest[:, layer * c : (layer + 1) * c]
    both = piece(9 * c) * whole_scale
    left[...] = both[:, 0:c]
    right[...] = both[:, c : 2 * c]
    at = pl.ds(pl.multiple_of((10 + place[1]) * c, c), c)
    offset[...] = total[at, :].astype(F32) * offset_scale


def per_device(features, left_weight, right_weight, offset_embed, kernels, dilation, cotangent):
    rows, c = features.shape
    group = offset_embed.shape[1]
    bins, band = lax.axis_size("bins"), lax.axis_size("band")
    devices = bins * band
    total_bins, total_band = rows * bins, group * band
    every = ("bins", "band")
    place = jnp.stack([lax.axis_index("bins"), lax.axis_index("band")]).astype(jnp.int32)

    def beside(block, axis, step):
        count = lax.axis_size(axis)
        return lax.ppermute(block, axis, [((i + step) % count, i) for i in range(count)])

    end = rows // RIM2 - 1
    row_block = (RIM2, c, group)
    everywhere, low, high = pl.pallas_call(
        functools.partial(greet_kernel, rows),
        grid=(1,),
        out_shape=(
            jax.ShapeDtypeStruct((bins, rows // 2, HALF), BF16),
            jax.ShapeDtypeStruct(row_block, BF16),
            jax.ShapeDtypeStruct(row_block, BF16),
        ),
        in_specs=[
            pl.BlockSpec((rows, c), lambda _: (0, 0)),
            pl.BlockSpec(row_block, lambda _: (0, 0, 0)),
            pl.BlockSpec(row_block, lambda _: (end, 0, 0)),
        ],
        out_specs=(
            pl.BlockSpec((bins, rows // 2, HALF), lambda _: (0, 0, 0)),
            pl.BlockSpec(row_block, lambda _: (0, 0, 0)),
            pl.BlockSpec(row_block, lambda _: (0, 0, 0)),
        ),
        compiler_params=pltpu.CompilerParams(vmem_limit_bytes=WHOLE),
        name="greet",
    )(features, cotangent, cotangent)
    feats = lax.all_to_all(everywhere, "bins", 0, 0, tiled=True)
    cot_up, cot_down = beside(high, "bins", -1), beside(low, "bins", 1)
    edge_shape = jax.ShapeDtypeStruct(((rows + 2 * RIM2) // 16 * c + c, HALF), BF16)
    to_lo, to_hi = pl.pallas_call(
        functools.partial(edge_kernel, rows, c),
        out_shape=(edge_shape, edge_shape),
        in_specs=[VMEM] * 4,
        out_specs=(VMEM,) * 2,
        compiler_params=pltpu.CompilerParams(vmem_limit_bytes=SMALL),
        name="edges",
    )(cot_up, cotangent, cot_down, offset_embed)
    from_lo = beside(to_hi, "band", -1)
    from_hi = beside(to_lo, "band", 1)

    taps = jnp.transpose(kernels, (0, 2, 4, 1, 3)).reshape(LAYERS, 3 * c, 3 * c)
    back_taps = jnp.transpose(kernels, (0, 2, 3, 1, 4)).reshape(LAYERS, 3 * c, 3 * c)

    pair_map, payload = middle(
        rows, c, group, total_bins, total_band, devices,
        (place, dilation, feats, cot_up, cotangent, cot_down, from_lo, from_hi, offset_embed,
         left_weight, right_weight, taps, back_taps),
    )
    parts = lax.all_to_all(payload, every, 0, 0, tiled=True)
    summed = jnp.sum(parts.astype(F32), axis=0)
    feature_part = summed[:4]
    share = jnp.broadcast_to(summed[None, 4:].astype(BF16), (devices, 4, HALF))
    total = lax.all_to_all(share, every, 0, 0, tiled=True).reshape(4 * devices, HALF)
    quarters = lax.all_gather(feature_part, "band")
    pairs = quarters.reshape(rows // 2, HALF)
    grad_features = jnp.concatenate([pairs[:, :c], pairs[:, c:]], 0) / math.sqrt(total_band)
    whole_scale = 1.0 / math.sqrt(total_bins * total_band)
    grad_left, grad_right, grad_offset, grad_kernels = pl.pallas_call(
        functools.partial(unpack_kernel, c, whole_scale, 1.0 / math.sqrt(total_bins)),
        out_shape=(
            jax.ShapeDtypeStruct((c, c), F32),
            jax.ShapeDtypeStruct((c, c), F32),
            jax.ShapeDtypeStruct((c, group), F32),
            jax.ShapeDtypeStruct((LAYERS, 3, 3, c, c), F32),
        ),
        in_specs=[SMEM, VMEM],
        out_specs=(VMEM,) * 4,
        compiler_params=pltpu.CompilerParams(vmem_limit_bytes=SMALL),
        name="unpack",
    )(place, total)
    return pair_map, grad_features, grad_left, grad_right, grad_offset, grad_kernels


def solution(mesh):
    return jax.shard_map(
        per_device,
        mesh=mesh,
        in_specs=(P("bins", None), P(), P(), P(None, "band"), P(), P(), P("bins", None, "band")),
        out_specs=(P("bins", None, "band"), P("bins", None), P(), P(), P(None, "band"), P()),
        check_vma=False,
    )
```
